32 devices in a mesh: rowpt: 8 (over y, x, core), colpt: 4 (over z).
Axes of the slice: x: 2, y: 2, z: 4, core: 2. Of those that a mesh axis runs over, the one named last changes fastest.
Arguments:
- x_pairs: float32 [4, 1024, 1024], P(None, 'rowpt', 'colpt'), may hold values from -6 to 6
- eps_val: float32 [1024], P('rowpt'), may hold values from -2 to -0.5
- eps_con: float32 [1024], P('colpt'), may hold values from 0.5 to 2
- orb_val: float32 [8192, 1024], P(('rowpt', 'colpt')), may hold values from -0.35 to 0.35
- orb_con: float32 [8192, 1024], P(('rowpt', 'colpt')), may hold values from -0.35 to 0.35
- screened_w: float32 [8192, 8192], P('rowpt', 'colpt'), may hold values from -0.0625 to 0.0625
Outputs:
- hx: float32 [4, 1024, 1024], P(None, 'rowpt', 'colpt')
The draws below stay inside these ranges and needn't reach their ends.
All inputs are finite; a program needn't handle non-finite values.
Results may differ from the reference program's by a relative error of at most 0.00005.
Values sent between devices are 32-bit elements; how exact they have to be, the bound alone decides.
No kernel may reach another device: no remote copies, remote signals or barrier semaphores. Data moves between devices by JAX's collectives and lax.ppermute only.
A program may use at most 64 MiB of HBM per device.

```python
import jax
import jax.numpy as jnp
from jax import lax

NV = 1024
NC = 1024
NP = 8192
B = 4


def level_of(rng, extent, split, least, top_value):
    factor_of, own = 1.0, jax.random.fold_in(rng, 6)
    for axis_at, shards_of in split:
        draws = jnp.exp(jax.random.uniform(jax.random.fold_in(own, axis_at), (shards_of,), jnp.float32, least / len(split), top_value / len(split)))
        factor_of = factor_of * jnp.repeat(draws, extent[axis_at] // shards_of).reshape([-1 if axis == axis_at else 1 for axis in range(len(extent))])
    return factor_of


def scatter_about(rng, dims, width, most, split=(), dtype=jnp.bfloat16):
    result = jax.random.normal(rng, dims, jnp.float32) * width
    if len(split) > 0:
        result = level_of(rng, dims, split, -0.22, 0.18) * result
    return jnp.clip(result, min=-most, max=most).astype(dtype)


def setup_inputs(seed: int = 0) -> dict:
    arg_keys = jax.random.split(jax.random.key(seed), 7)
    x_pairs = scatter_about(arg_keys[0], (B, NV, NC), 1.0, 6.0, ((1, 8), (2, 4)), jnp.float32)
    eps_val = jnp.clip(-2.0 + 1.5 * jax.random.uniform(arg_keys[1], (NV,), jnp.float32) ** level_of(arg_keys[1], (NV,), ((0, 8),), -0.2, 0.2), -2.0, -0.5)
    eps_con = jnp.clip(0.5 + 1.5 * jax.random.uniform(arg_keys[2], (NC,), jnp.float32) ** level_of(arg_keys[2], (NC,), ((0, 4),), -0.2, 0.2), 0.5, 2.0)
    orb_val = scatter_about(arg_keys[3], (NP, NV), 0.053, 0.35, ((0, 32),), jnp.float32)
    orb_con = scatter_about(arg_keys[4], (NP, NC), 0.053, 0.35, ((0, 32),), jnp.float32)
    screened_w = scatter_about(arg_keys[5], (NP, NP), NP ** -0.5, 0.0625, ((0, 8), (1, 4)), jnp.float32)
    return {"x_pairs": x_pairs, "eps_val": eps_val, "eps_con": eps_con, "orb_val": orb_val, "orb_con": orb_con, "screened_w": screened_w}


def reference(x_pairs, eps_val, eps_con, orb_val, orb_con, screened_w):
    def density_one(x_one):
        through = jnp.dot(orb_con, x_one.T, precision=lax.Precision.HIGHEST)
        return jnp.sum(through * orb_val, axis=1)

    density = lax.map(density_one, x_pairs)
    screened = jnp.dot(density, screened_w.T, precision=lax.Precision.HIGHEST)

    def kernel_one(pot_one):
        weighted = orb_val * pot_one[:, None]
        return jnp.dot(weighted.T, orb_con, precision=lax.Precision.HIGHEST)

    kernel = lax.map(kernel_one, screened)
    diff = eps_con[None, None, :] - eps_val[None, :, None]
    return diff * x_pairs + kernel
```

```python
import jax
import jax.numpy as jnp
from jax import lax
from jax.sharding import Mesh, PartitionSpec as P

HIGH = lax.Precision.HIGH


def swap(x, axis, size, mask):
    return lax.ppermute(x, axis, [(i, i ^ mask) for i in range(size)])


def relative(x, axis, index):
    size = x.shape[axis]
    bit = 1
    while bit < size:
        shape = x.shape[:axis] + (size // (2 * bit), 2, bit) + x.shape[axis + 1:]
        flipped = jnp.flip(x.reshape(shape), axis + 1).reshape(x.shape)
        x = jnp.where((index & bit) != 0, flipped, x)
        bit *= 2
    return x


def make(nchip, ntop):
    def rc_swap(x, mask):
        return swap(x, "rc", nchip, mask)

    def top_swap(x, mask):
        return swap(x, "top", ntop, mask)

    def pair_swap(x):
        return swap(x, "pair", 2, 1)

    def core_swap(x):
        return swap(x, "core", 2, 1)

    def gather_chips(native):
        out = {0: native}
        half = native.shape[0] // 2
        for j in range(1, nchip):
            low = j & -j
            high = 1 << (j.bit_length() - 1)
            if low == high:
                out[j] = rc_swap(native, j)
            else:
                first = rc_swap(out[j ^ high][:half], high)
                second = rc_swap(out[j ^ low][half:], low)
                out[j] = jnp.concatenate([first, second], axis=0)
        return [out[j] for j in range(nchip)]

    def per_device(x_pairs, eps_val, eps_con, orb_val, orb_con, screened_w):
        rc = lax.axis_index("rc")
        core = lax.axis_index("core")
        top = lax.axis_index("top")
        pair = lax.axis_index("pair")
        nb, nv, nc = x_pairs.shape
        pts = orb_val.shape[0]

        parts = [x_pairs] + [top_swap(x_pairs, a) for a in range(1, ntop)]
        x_own = jnp.concatenate(parts, axis=2)
        x_other = core_swap(x_own)
        x_all = jnp.where(core == 0, jnp.stack([x_own, x_other], 1), jnp.stack([x_other, x_own], 1))
        x_all = x_all.reshape(nb * 2 * nv, ntop * nc)

        con = orb_con.reshape(pts, ntop, 2, nc)
        con_mine = jnp.where(pair == 0, con[:, :, 0], con[:, :, 1])
        con_theirs = jnp.where(pair == 0, con[:, :, 1], con[:, :, 0])
        con_mine = relative(con_mine, 1, top).reshape(pts, ntop * nc)
        con_theirs = relative(con_theirs, 1, top).reshape(pts, ntop * nc)
        con_next = pair_swap(con_theirs)
        con_blocks = [gather_chips(con_mine), gather_chips(con_next)]

        val_t = orb_val.T.reshape(nchip, 2 * nv, pts)
        val_here = []
        for j in range(nchip):
            piece = lax.dynamic_index_in_dim(val_t, rc ^ j, 0, keepdims=False)
            val_here.append(piece if j == 0 else rc_swap(piece, j))
        val_next = [pair_swap(piece) for piece in val_here]
        val_blocks = [val_here, val_next]

        dens = []
        for e in range(2):
            for j in range(nchip):
                through = lax.dot_general(
                    x_all, con_blocks[e][j], (((1,), (1,)), ((), ())), precision=HIGH
                ).reshape(nb, 2 * nv, pts)
                dens.append(jnp.sum(through * val_blocks[e][j][None], axis=1))
        dens = jnp.stack(dens, 0).reshape(2, nchip, nb, pts)

        by_rc = relative(dens, 1, rc).reshape(2, ntop, 2, nb, pts)
        by_pair = [
            jnp.where(pair == 0, by_rc[:, :, 0], by_rc[:, :, 1]),
            jnp.where(pair == 0, by_rc[:, :, 1], by_rc[:, :, 0]),
        ]
        total = by_pair[0]
        for a in range(1, nchip):
            total = total + rc_swap(by_pair[0], a)
        across = by_pair[1]
        sent = swap2(across, nchip)
        for piece in sent:
            total = total + piece[::-1]
        total = relative(total, 1, top)
        cols = [total[:, 0]] + [top_swap(total[:, a], a) for a in range(1, ntop)]
        cols = jnp.stack(cols, 0)
        cols = relative(relative(cols, 0, top), 1, pair)
        other = core_swap(cols)
        both = jnp.where(core == 0, jnp.stack([cols, other], 0), jnp.stack([other, cols], 0))
        density = jnp.transpose(both.reshape(-1, nb, pts), (1, 0, 2)).reshape(nb, -1)

        part = lax.dot_general(density, screened_w, (((1,), (1,)), ((), ())), precision=HIGH)
        part = jnp.transpose(part.reshape(nb, ntop, 2, pts), (1, 2, 0, 3))
        part = relative(relative(part, 0, top), 1, pair)
        row = part[0] + swap_pt(part[0], ntop, 0, True)[::-1]
        for a in range(1, ntop):
            row = row + swap_pt(part[a], ntop, a, False) + swap_pt(part[a], ntop, a, True)[::-1]
        pot = jnp.stack([row] + [rc_swap(row, j) for j in range(1, nchip)], 1)
        pot = jnp.transpose(pot, (2, 0, 1, 3)).reshape(nb, -1)

        val_all = jnp.concatenate(val_here + val_next, axis=1)
        con_all = jnp.concatenate(con_blocks[0] + con_blocks[1], axis=0)
        weighted = (val_all[None] * pot[:, None, :]).reshape(nb, 2, nv, -1)
        mine = jnp.where(core == 0, weighted[:, 0], weighted[:, 1]).reshape(nb * nv, -1)
        yours = jnp.where(core == 0, weighted[:, 1], weighted[:, 0]).reshape(nb * nv, -1)
        kernel = None
        for a in list(range(1, ntop)) + [0]:
            con_a = con_all[:, a * nc:(a + 1) * nc]
            away = core_swap(jnp.dot(yours, con_a, precision=HIGH))
            step = jnp.dot(mine, con_a, precision=HIGH) + away
            if a:
                step = top_swap(step, a)
            kernel = step if kernel is None else kernel + step
        diff = eps_con[None, None, :] - eps_val[None, :, None]
        return diff * x_pairs + kernel.reshape(nb, nv, nc)

    def swap2(x, n):
        return [
            lax.ppermute(x, ("rc", "pair"), [(r * 2 + p, (r ^ a) * 2 + (p ^ 1)) for r in range(n) for p in range(2)])
            for a in range(n)
        ]

    def swap_pt(x, n, a, flip):
        return lax.ppermute(
            x,
            ("top", "pair"),
            [(t * 2 + p, (t ^ a) * 2 + (p ^ int(flip))) for t in range(n) for p in range(2)],
        )

    return per_device


def solution(mesh):
    nrow, ncol = mesh.shape["rowpt"], mesh.shape["colpt"]
    nchip, ntop = nrow // 2, ncol // 2
    fine = Mesh(mesh.devices.reshape(nchip, 2, ntop, 2), ("rc", "core", "top", "pair"))
    row, col = ("rc", "core"), ("top", "pair")
    in_specs = (P(None, row, col), P(row), P(col), P(row + col, None), P(row + col, None), P(row, col))
    return jax.shard_map(
        make(nchip, ntop), mesh=fine, in_specs=in_specs, out_specs=P(None, row, col), check_vma=False
    )
```

```python
import functools

import jax
import jax.numpy as jnp
from jax import lax
from jax.experimental import pallas as pl
from jax.experimental.pallas import tpu as pltpu
from jax.sharding import Mesh, PartitionSpec as P

HIGH = lax.Precision.HIGH
VMEM = pl.BlockSpec(memory_space=pltpu.VMEM)
SMEM = pl.BlockSpec(memory_space=pltpu.SMEM)
PARAMS = pltpu.CompilerParams(vmem_limit_bytes=14 * 1024 * 1024)


def swap(x, axis, size, mask):
    return lax.ppermute(x, axis, [(i, i ^ mask) for i in range(size)])


def relative(x, axis, index):
    size = x.shape[axis]
    bit = 1
    while bit < size:
        shape = x.shape[:axis] + (size // (2 * bit), 2, bit) + x.shape[axis + 1:]
        flipped = jnp.flip(x.reshape(shape), axis + 1).reshape(x.shape)
        x = jnp.where((index & bit) != 0, flipped, x)
        bit *= 2
    return x


def single(j):
    return j & (j - 1) == 0


def split(x):
    high = x.astype(jnp.bfloat16)
    return high, (x - high.astype(jnp.float32)).astype(jnp.bfloat16)


def pack_kernel(nchip, ntop, where, con_ref, val_ref, pair_ref, *outs):
    pts, nc = pair_ref.shape[1:]
    rc, top, pair = where[0], where[1], where[2]

    def con_tile(a, e):
        at = ((top ^ a) * 2 + (pair ^ e)) * nc
        return con_ref[:, pl.ds(pl.multiple_of(at, nc), nc)]

    def val_tile(j):
        at = (rc ^ j) * nc
        return val_ref[:, pl.ds(pl.multiple_of(at, nc), nc)].T

    for a in range(ntop):
        pair_ref[a] = con_tile(a, 1)
    pair_ref[ntop] = val_tile(0)
    for j in range(1, nchip):
        out = outs[j - 1]
        if single(j):
            for a in range(ntop):
                out[a] = con_tile(a, 0)
        out[out.shape[0] - 1] = val_tile(j)


def pack(nchip, ntop, aligned, rc, top, pair, orb_con, orb_val, nc):
    pts = orb_con.shape[0]
    if aligned:
        sizes = [ntop + 1] + [ntop + 1 if single(j) else 1 for j in range(1, nchip)]
        return pl.pallas_call(
            functools.partial(pack_kernel, nchip, ntop),
            out_shape=[jax.ShapeDtypeStruct((s, pts, nc), jnp.float32) for s in sizes],
            in_specs=[SMEM, VMEM, VMEM],
            out_specs=[VMEM] * nchip,
            compiler_params=PARAMS,
        )(jnp.stack([rc, top, pair]).astype(jnp.int32), orb_con, orb_val)

    def con_tile(a, e):
        return lax.dynamic_slice_in_dim(orb_con, ((top ^ a) * 2 + (pair ^ e)) * nc, nc, 1)

    def val_tile(j):
        return lax.dynamic_slice_in_dim(orb_val, (rc ^ j) * nc, nc, 1).T.reshape(pts, nc)

    out = [jnp.stack([con_tile(a, 1) for a in range(ntop)] + [val_tile(0)])]
    for j in range(1, nchip):
        con = [con_tile(a, 0) for a in range(ntop)] if single(j) else []
        out.append(jnp.stack(con + [val_tile(j)]))
    return out


def operands(tiles):
    arrays, at = [], []
    for array, index in tiles:
        where = [i for i, other in enumerate(arrays) if other is array]
        if not where:
            arrays.append(array)
            where = [len(arrays) - 1]
        at.append((where[0], index))
    return arrays, at


def density_kernel(nblk, ntop, nin, con_at, val_at, core_ref, *refs):
    x = refs[:2 * ntop]
    tiles = refs[2 * ntop:2 * ntop + nin]
    dens_ref = refs[2 * ntop + nin]
    keep = refs[2 * ntop + nin + 1:-2]
    left, right = refs[-2:]
    nb, nv, nc = x[0].shape
    core = core_ref[0]
    for a in range(ntop):
        for k in range(2):
            high, low = split(x[a * 2 + k][...].reshape(nb * nv, nc))
            rows = pl.ds(k * nb * nv, nb * nv)
            left[rows, pl.ds(a * nc, nc)] = high
            left[rows, pl.ds((ntop + a) * nc, nc)] = high
            left[rows, pl.ds((2 * ntop + a) * nc, nc)] = low
    for g in range(nblk):
        for a in range(ntop):
            array, index = con_at[g * ntop + a]
            high, low = split(tiles[array][index])
            keep[g][a, 0] = high
            keep[g][a, 1] = low
            right[g, :, pl.ds(a * nc, nc)] = high
            right[g, :, pl.ds((ntop + a) * nc, nc)] = low
            right[g, :, pl.ds((2 * ntop + a) * nc, nc)] = high
        through = lax.dot_general(
            left[...], right[g], (((1,), (1,)), ((), ())), preferred_element_type=jnp.float32
        )
        pts = through.shape[1]
        array, index = val_at[g]
        total = None
        for k in range(2):
            rows = tiles[array][index, pl.ds(pl.multiple_of((core ^ k) * nv, nv), nv), :]
            part = through[k * nb * nv:(k + 1) * nb * nv].reshape(nb, nv, pts) * rows[None]
            part = jnp.sum(part, axis=1)
            total = part if total is None else total + part
        dens_ref[g] = total


def densities(aligned, core, x, con, val):
    nblk, ntop = len(con), len(x)
    nb, nv, nc = x[0][0].shape
    if aligned:
        arrays, at = operands([t for row in con for t in row] + list(val))
        pts = arrays[0].shape[1]
        outs = pl.pallas_call(
            functools.partial(density_kernel, nblk, ntop, len(arrays), at[:nblk * ntop], at[nblk * ntop:]),
            out_shape=[jax.ShapeDtypeStruct((nblk, nb, pts), jnp.float32)]
            + [jax.ShapeDtypeStruct((ntop, 2, pts, nc), jnp.bfloat16)] * nblk,
            in_specs=[SMEM] + [VMEM] * (2 * ntop + len(arrays)),
            out_specs=[VMEM] * (nblk + 1),
            scratch_shapes=[
                pltpu.VMEM((2 * nb * nv, 3 * ntop * nc), jnp.bfloat16),
                pltpu.VMEM((nblk, pts, 3 * ntop * nc), jnp.bfloat16),
            ],
            compiler_params=PARAMS,
            cost_estimate=pl.CostEstimate(
                flops=2 * nblk * 2 * nb * nv * pts * 3 * ntop * nc, bytes_accessed=nblk * 2 ** 20, transcendentals=0
            ),
        )(core.astype(jnp.int32)[None], *[t for row in x for t in row], *arrays)
        return [outs[0][g] for g in range(nblk)], list(outs[1:])
    tiles = [jnp.where(core == 0, jnp.stack(row, 1), jnp.stack(row[::-1], 1)) for row in x]
    con = [[array[index] for array, index in row] for row in con]
    out = []
    for g in range(nblk):
        through = 0.0
        for a in range(ntop):
            through = through + jnp.einsum("bkvc,pc->bkvp", tiles[a], con[g][a], precision=HIGH)
        array, index = val[g]
        out.append(jnp.sum(through * array[index].reshape(1, 2, nv, -1), axis=(1, 2)))
    return out, con


def apply_kernel(nblk, nin, a, k, val_at, core_ref, pot_ref, *refs):
    val = refs[:nin]
    con = refs[nin:nin + nblk]
    out_ref, left, right = refs[nin + nblk:]
    nb, nv, nc = out_ref.shape
    pts = con[0].shape[2]
    core = core_ref[0]
    for g in range(nblk):
        array, index = val_at[g]
        rows = val[array][index, pl.ds(pl.multiple_of((core ^ k) * nv, nv), nv), :]
        for b in range(nb):
            high, low = split(rows * pot_ref[g, pl.ds(b, 1), :])
            at = pl.ds(b * nv, nv)
            left[at, pl.ds(3 * g * pts, pts)] = high
            left[at, pl.ds((3 * g + 1) * pts, pts)] = high
            left[at, pl.ds((3 * g + 2) * pts, pts)] = low
        right[pl.ds(3 * g * pts, pts), :] = con[g][a, 0]
        right[pl.ds((3 * g + 1) * pts, pts), :] = con[g][a, 1]
        right[pl.ds((3 * g + 2) * pts, pts), :] = con[g][a, 0]
    total = jnp.dot(left[...], right[...], preferred_element_type=jnp.float32)
    out_ref[...] = total.reshape(nb, nv, nc)


def applied(aligned, core, pot, val, con, a, k, shape):
    nb, nv, nc = shape
    nblk = len(val)
    if aligned:
        pts = pot.shape[2]
        arrays, at = operands(val)
        return pl.pallas_call(
            functools.partial(apply_kernel, nblk, len(arrays), a, k, at),
            out_shape=jax.ShapeDtypeStruct(shape, jnp.float32),
            in_specs=[SMEM] + [VMEM] * (1 + len(arrays) + nblk),
            out_specs=VMEM,
            scratch_shapes=[
                pltpu.VMEM((nb * nv, 3 * nblk * pts), jnp.bfloat16),
                pltpu.VMEM((3 * nblk * pts, nc), jnp.bfloat16),
            ],
            compiler_params=PARAMS,
            cost_estimate=pl.CostEstimate(
                flops=2 * nb * nv * 3 * nblk * pts * nc, bytes_accessed=4 * 2 ** 20, transcendentals=0
            ),
        )(core.astype(jnp.int32)[None], pot, *arrays, *con)
    out = 0.0
    for g in range(nblk):
        array, index = val[g]
        rows = lax.dynamic_slice_in_dim(array[index].reshape(2 * nv, -1), (core ^ k) * nv, nv, 0)
        out = out + jnp.einsum("vp,bp,pc->bvc", rows, pot[g], con[g][a], precision=HIGH)
    return out


def make(nchip, ntop):
    def rc_swap(x, mask):
        return swap(x, "rc", nchip, mask)

    def top_swap(x, mask):
        return swap(x, "top", ntop, mask)

    def pair_swap(x):
        return swap(x, "pair", 2, 1)

    def core_swap(x):
        return swap(x, "core", 2, 1)

    def col_swap(x, mask):
        n = 2 * ntop
        return lax.ppermute(x, ("top", "pair"), [(i, i ^ mask) for i in range(n)])

    def relay(tiles, j):
        high = 1 << (j.bit_length() - 1)
        low = j & -j
        out = []
        for a in range(ntop):
            mask = low if a % 2 else high
            array, index = tiles[j ^ mask][a]
            out.append((rc_swap(array[index:index + 1], mask), 0))
        return out

    def per_device(x_pairs, eps_val, eps_con, orb_val, orb_con, screened_w):
        rc = lax.axis_index("rc")
        core = lax.axis_index("core")
        top = lax.axis_index("top")
        pair = lax.axis_index("pair")
        nb, nv, nc = x_pairs.shape
        pts = orb_val.shape[0]
        aligned = nc % 128 == 0 and pts == nc and 2 * nv == nc

        packed = pack(nchip, ntop, aligned, rc, top, pair, orb_con, orb_val, nc)
        from_pair = pair_swap(packed[0])
        from_chip = {j: rc_swap(packed[j], j) for j in range(1, nchip)}
        x_tops = [x_pairs] + [top_swap(x_pairs, a) for a in range(1, ntop)]
        x_tops = lax.optimization_barrier(x_tops)
        x = [[t, core_swap(t)] for t in x_tops]

        val = [{0: (packed[0], ntop)}, {0: (from_pair, ntop)}]
        con = [{0: [(packed[1], a) for a in range(ntop)]}, {0: [(from_pair, a) for a in range(ntop)]}]
        for j in range(1, nchip):
            val[0][j] = (from_chip[j], from_chip[j].shape[0] - 1)
            if single(j):
                con[0][j] = [(from_chip[j], a) for a in range(ntop)]

        def take(tiles):
            return jnp.stack([array[index] for array, index in tiles])

        if nchip == 4:
            con[0][3] = [None] * ntop
            for mask in (2, 1):
                mine = [a for a in range(ntop) if (a % 2 == 0) == (mask == 2)]
                got = rc_swap(take([con[0][3 ^ mask][a] for a in mine] + con[1][0]), mask)
                for i, a in enumerate(mine):
                    con[0][3][a] = (got, i)
                con[1][mask] = [(got, len(mine) + a) for a in range(ntop)]
        else:
            for j in range(1, nchip):
                if single(j):
                    got = rc_swap(take(con[1][0]), j)
                    con[1][j] = [(got, a) for a in range(ntop)]
        val_pair = pair_swap(take([val[0][j] for j in range(1, nchip)]))
        for j in range(1, nchip):
            val[1][j] = (val_pair, j - 1)
        for e in range(2):
            for j in range(1, nchip):
                if j not in con[e]:
                    con[e][j] = relay(con[e], j)

        groups = [
            [(0, 0)] + [(0, j) for j in range(1, nchip) if single(j)] + [(1, 0)],
            [(0, j) for j in range(1, nchip) if not single(j)] + [(1, j) for j in range(1, nchip) if single(j)],
            [(1, j) for j in range(1, nchip) if not single(j)],
        ]
        dens, kept = {}, {}
        for group in groups:
            if group:
                d, kc = densities(aligned, core, x, [con[e][j] for e, j in group], [val[e][j] for e, j in group])
                dens.update(zip(group, d))
                kept.update(zip(group, kc))
        order = [(e, j) for e in range(2) for j in range(nchip)]
        part = jnp.stack([dens[at] for at in order], 0).reshape(2, nchip, nb, pts)

        part = relative(relative(part, 1, rc ^ (top * 2 + pair)), 0, pair)
        got = [part[:, 0]] + [col_swap(part[:, d], d) for d in range(1, nchip)]
        part = jnp.stack([got[2 * d] + got[2 * d + 1] for d in range(ntop)])
        part = relative(part, 0, top)
        total = part
        for a in range(1, nchip):
            total = total + rc_swap(part, a)
        other = core_swap(total)
        both = jnp.where(core == 0, jnp.stack([total, other]), jnp.stack([other, total]))
        density = jnp.transpose(both.reshape(-1, nb, pts), (1, 0, 2)).reshape(nb, -1)

        rows = lax.dot_general(density, screened_w, (((1,), (1,)), ((), ())), precision=HIGH)
        rows = jnp.transpose(rows.reshape(nb, ntop, 2, pts), (1, 2, 0, 3))
        rows = relative(rows, 0, top)
        row = rows[0]
        for d in range(1, nchip):
            row = row + col_swap(rows[d // 2], d)
        row = relative(row, 0, pair)
        pot = jnp.stack([row] + [rc_swap(row, j) for j in range(1, nchip)], 1).reshape(2 * nchip, nb, pts)

        vals = [val[e][j] for e, j in order]
        cons = [kept[at] for at in order]
        kernel = None
        for a in list(range(1, ntop)) + [0]:
            away = core_swap(applied(aligned, core, pot, vals, cons, a, 1, x_pairs.shape))
            step = applied(aligned, core, pot, vals, cons, a, 0, x_pairs.shape) + away
            if a:
                step, pot = lax.optimization_barrier((step, pot))
                step = top_swap(step, a)
            kernel = step if kernel is None else kernel + step
        diff = eps_con[None, None, :] - eps_val[None, :, None]
        return diff * x_pairs + kernel

    return per_device


def solution(mesh):
    nrow, ncol = mesh.shape["rowpt"], mesh.shape["colpt"]
    nchip, ntop = nrow // 2, ncol // 2
    fine = Mesh(mesh.devices.reshape(nchip, 2, ntop, 2), ("rc", "core", "top", "pair"))
    row, col = ("rc", "core"), ("top", "pair")
    in_specs = (P(None, row, col), P(row), P(col), P(row + col, None), P(row + col, None), P(row, col))
    return jax.shard_map(
        make(nchip, ntop), mesh=fine, in_specs=in_specs, out_specs=P(None, row, col), check_vma=False
    )
```

```python
import functools

import jax
import jax.numpy as jnp
from jax import lax
from jax.experimental import pallas as pl
from jax.experimental.pallas import tpu as pltpu
from jax.sharding import Mesh, PartitionSpec as P

HIGH = lax.Precision.HIGH
VMEM = pl.BlockSpec(memory_space=pltpu.VMEM)
ANY = pl.BlockSpec(memory_space=pl.ANY)
SMEM = pl.BlockSpec(memory_space=pltpu.SMEM)
COST = pl.CostEstimate(flops=2 * 10**9, bytes_accessed=4 * 2**20, transcendentals=0)
PARAMS = pltpu.CompilerParams(vmem_limit_bytes=14 * 1024 * 1024)


def swap(x, axis, size, mask):
    return lax.ppermute(x, axis, [(i, i ^ mask) for i in range(size)])


def relative(x, axis, index):
    size = x.shape[axis]
    bit = 1
    while bit < size:
        shape = x.shape[:axis] + (size // (2 * bit), 2, bit) + x.shape[axis + 1:]
        flipped = jnp.flip(x.reshape(shape), axis + 1).reshape(x.shape)
        x = jnp.where((index & bit) != 0, flipped, x)
        bit *= 2
    return x


def ordered(first, then):
    return lax.optimization_barrier((first, then))


def single(j):
    return j & (j - 1) == 0


def split(x):
    high = x.astype(jnp.bfloat16)
    return high, (x - high.astype(jnp.float32)).astype(jnp.bfloat16)


def pack_kernel(nchip, ntop, where, con_ref, val_ref, *outs):
    nc = outs[0].shape[2]
    rc, top, pair = where[0], where[1], where[2]

    def con_tile(a, e):
        at = ((top ^ a) * 2 + (pair ^ e)) * nc
        return con_ref[:, pl.ds(pl.multiple_of(at, nc), nc)]

    def val_tile(j):
        at = (rc ^ j) * nc
        return val_ref[:, pl.ds(pl.multiple_of(at, nc), nc)].T

    for j in range(nchip + 1):
        out = outs[j]
        if j == 0 or (j < nchip and single(j)):
            for a in range(ntop):
                out[a] = con_tile(a, int(j == 0))
        if j:
            out[out.shape[0] - 1] = val_tile(j % nchip)


def pack(nchip, ntop, aligned, rc, top, pair, orb_con, orb_val, nc):
    pts = orb_con.shape[0]
    if aligned:
        sizes = [ntop] + [ntop + 1 if single(j) else 1 for j in range(1, nchip)] + [1]
        return pl.pallas_call(
            functools.partial(pack_kernel, nchip, ntop),
            out_shape=[jax.ShapeDtypeStruct((s, pts, nc), jnp.float32) for s in sizes],
            in_specs=[SMEM, VMEM, VMEM],
            out_specs=[VMEM] * (nchip + 1),
            compiler_params=PARAMS,
            cost_estimate=COST,
        )(jnp.stack([rc, top, pair]).astype(jnp.int32), orb_con, orb_val)

    def con_tile(a, e):
        return lax.dynamic_slice_in_dim(orb_con, ((top ^ a) * 2 + (pair ^ e)) * nc, nc, 1)

    def val_tile(j):
        return lax.dynamic_slice_in_dim(orb_val, (rc ^ j) * nc, nc, 1).T.reshape(pts, nc)

    out = [jnp.stack([con_tile(a, 1) for a in range(ntop)])]
    for j in range(1, nchip):
        con = [con_tile(a, 0) for a in range(ntop)] if single(j) else []
        out.append(jnp.stack(con + [val_tile(j)]))
    return out + [val_tile(0)[None]]


def operands(tiles):
    arrays, at = [], []
    for array, index in tiles:
        where = [i for i, other in enumerate(arrays) if other is array]
        if not where:
            arrays.append(array)
            where = [len(arrays) - 1]
        at.append((where[0], index))
    return arrays, at


def halves_kernel(x_refs, out_ref):
    nb, nv, nc = x_refs[0].shape
    width = out_ref.shape[1] // 2
    for i, ref in enumerate(x_refs):
        a, k = i // 2, i % 2
        high, low = split(ref[...].reshape(nb * nv, nc))
        rows = pl.ds(k * nb * nv, nb * nv)
        out_ref[rows, pl.ds(a * nc, nc)] = high
        out_ref[rows, pl.ds(width + a * nc, nc)] = low


def halves(x):
    flat = [t for row in x for t in row]
    nb, nv, nc = flat[0].shape
    return pl.pallas_call(
        lambda *refs: halves_kernel(refs[:-1], refs[-1]),
        out_shape=jax.ShapeDtypeStruct((2 * nb * nv, 2 * len(x) * nc), jnp.bfloat16),
        in_specs=[VMEM] * len(flat),
        out_specs=VMEM,
        compiler_params=PARAMS,
        cost_estimate=COST,
    )(*flat)


def density_kernel(nblk, ntop, shape, con_at, val_at, core_ref, x_ref, *refs):
    tiles, (dens_ref, right) = refs[:-2], refs[-2:]
    nb, nv, nc = shape
    width = ntop * nc
    core = core_ref[0]
    for g in range(nblk):
        for a in range(ntop):
            array, index = con_at[g * ntop + a]
            high, low = split(tiles[array][index])
            right[g, :, pl.ds(a * nc, nc)] = high
            right[g, :, pl.ds(width + a * nc, nc)] = high
            right[g, :, pl.ds(2 * width + a * nc, nc)] = low
        array, index = val_at[g]
        total = None
        for k in range(2):
            at = pl.ds(k * nb * nv, nb * nv)
            left = jnp.concatenate([x_ref[at, :], x_ref[at, pl.ds(0, width)]], axis=1)
            through = lax.dot_general(
                left, right[g], (((1,), (1,)), ((), ())), preferred_element_type=jnp.float32
            )
            rows = tiles[array][index, pl.ds(pl.multiple_of((core ^ k) * nv, nv), nv), :]
            part = jnp.sum(through.reshape(nb, nv, -1) * rows[None], axis=1)
            total = part if total is None else total + part
        dens_ref[g] = total


def densities(aligned, core, shape, x, con, val):
    nblk, ntop = len(con), len(con[0])
    nb, nv, nc = shape
    if aligned:
        arrays, at = operands([t for row in con for t in row] + list(val))
        pts = arrays[0].shape[1]
        return pl.pallas_call(
            functools.partial(density_kernel, nblk, ntop, shape, at[:nblk * ntop], at[nblk * ntop:]),
            out_shape=jax.ShapeDtypeStruct((nblk, nb, pts), jnp.float32),
            in_specs=[SMEM] + [VMEM] * (1 + len(arrays)),
            out_specs=VMEM,
            scratch_shapes=[pltpu.VMEM((nblk, pts, 3 * ntop * nc), jnp.bfloat16)],
            compiler_params=PARAMS,
            cost_estimate=COST,
        )(core.astype(jnp.int32)[None], x, *arrays)
    out = []
    for g in range(nblk):
        through = 0.0
        for a in range(ntop):
            array, index = con[g][a]
            through = through + jnp.einsum("bkvc,pc->bkvp", x[a], array[index], precision=HIGH)
        array, index = val[g]
        out.append(jnp.sum(through * array[index].reshape(1, 2, nv, -1), axis=(1, 2)))
    return jnp.stack(out)


def route_kernel(order, nchip, where, *refs):
    groups, out_ref, held = refs[:-2], refs[-2], refs[-1]
    nb = held.shape[1]
    rc, pair = where[0], where[1]
    at = 0
    for ref in groups:
        for g in range(ref.shape[0]):
            held[order[at]] = ref[g]
            at += 1
    for z in range(nchip):
        for p in range(2):
            piece = held[(pair ^ p) * nchip + (rc ^ z)]
            for d in range(out_ref.shape[0] // nchip):
                out_ref[d * nchip + z, pl.ds(p * nb, nb), :] = piece


def route(aligned, nchip, rc, pair, order, groups):
    nb, pts = groups[0].shape[1:]
    if aligned:
        return pl.pallas_call(
            functools.partial(route_kernel, order, nchip),
            out_shape=jax.ShapeDtypeStruct((2 * nchip * nchip, 2 * nb, pts), jnp.float32),
            in_specs=[SMEM] + [VMEM] * len(groups),
            out_specs=VMEM,
            scratch_shapes=[pltpu.VMEM((2 * nchip, nb, pts), jnp.float32)],
            compiler_params=PARAMS,
            cost_estimate=COST,
        )(jnp.stack([rc, pair]).astype(jnp.int32), *groups)
    flat = jnp.concatenate(groups)
    flat = jnp.stack([flat[order.index(i)] for i in range(2 * nchip)]).reshape(2, nchip, nb, pts)
    flat = jnp.transpose(relative(relative(flat, 1, rc), 0, pair), (1, 0, 2, 3)).reshape(nchip, 2 * nb, pts)
    return jnp.tile(flat, (2 * nchip, 1, 1))


def screen_kernel(nchip, ntop, top_ref, got_ref, w_ref, *refs):
    outs, (dens, left) = refs[:ntop], refs[ntop:]
    nb = got_ref.shape[1] // 2
    pts = got_ref.shape[2]
    top = top_ref[0]
    for k in range(2):
        for t in range(ntop):
            total = None
            for r in range(nchip):
                for p in range(2):
                    piece = got_ref[((r * 2 + k) * ntop + t) * 2 + p]
                    total = piece if total is None else total + piece
            for p in range(2):
                dens[:, pl.ds(((k * ntop + t) * 2 + p) * pts, pts)] = total[p * nb:(p + 1) * nb]
    high, low = split(dens[...])
    left[...] = jnp.zeros_like(left)
    left[pl.ds(0, nb), :] = high
    left[pl.ds(nb, nb), :] = low
    for a in range(ntop):
        for p in range(2):
            at = pl.multiple_of(((top ^ a) * 2 + p) * pts, pts)
            high, low = split(w_ref[pl.ds(at, pts), :])
            dims = (((1,), (1,)), ((), ()))
            total = lax.dot_general(left[...], high, dims, preferred_element_type=jnp.float32)
            extra = lax.dot_general(left[...], low, dims, preferred_element_type=jnp.float32)
            outs[a][pl.ds(p * nb, nb), :] = total[:nb] + total[nb:2 * nb] + extra[:nb]


def screen(aligned, nchip, ntop, top, got, screened_w):
    nb, pts = got.shape[1] // 2, got.shape[2]
    if aligned:
        nq = screened_w.shape[1]
        return pl.pallas_call(
            functools.partial(screen_kernel, nchip, ntop),
            out_shape=[jax.ShapeDtypeStruct((2 * nb, pts), jnp.float32)] * ntop,
            in_specs=[SMEM, VMEM, VMEM],
            out_specs=[VMEM] * ntop,
            scratch_shapes=[pltpu.VMEM((nb, nq), jnp.float32), pltpu.VMEM((16, nq), jnp.bfloat16)],
            compiler_params=PARAMS,
            cost_estimate=COST,
        )(top.astype(jnp.int32)[None], got, screened_w)
    density = jnp.sum(got.reshape(nchip, 2, ntop, 2, 2, nb, pts), axis=(0, 3))
    density = jnp.transpose(density.reshape(-1, nb, pts), (1, 0, 2)).reshape(nb, -1)
    rows = lax.dot_general(density, screened_w, (((1,), (1,)), ((), ())), precision=HIGH)
    rows = jnp.transpose(rows.reshape(nb, ntop, 2, pts), (1, 2, 0, 3)).reshape(ntop, 2 * nb, pts)
    rows = relative(rows, 0, top)
    return [rows[a] for a in range(ntop)]


def gather_kernel(ntop, nin, con_at, val_at, core_ref, *refs):
    tiles, rights, val_refs = refs[:nin], refs[nin:nin + ntop], refs[nin + ntop:]
    nblk, nv, pts = val_refs[0].shape
    core = core_ref[0]
    for g in range(nblk):
        for a in range(ntop):
            array, index = con_at[a * nblk + g]
            high, low = split(tiles[array][index])
            rights[a][pl.ds(3 * g * pts, pts), :] = high
            rights[a][pl.ds((3 * g + 1) * pts, pts), :] = low
            rights[a][pl.ds((3 * g + 2) * pts, pts), :] = high
        array, index = val_at[g]
        for k in range(2):
            val_refs[k][g] = tiles[array][index, pl.ds(pl.multiple_of((core ^ k) * nv, nv), nv), :]


def gathered(aligned, core, after, val, con, nv):
    nblk, ntop = len(val), len(con)
    arrays, at = operands([t for row in con for t in row] + val)
    after, *arrays = lax.optimization_barrier((after, *arrays))
    tiles = [(arrays[i], index) for i, index in at]
    if aligned:
        _, pts, nc = arrays[0].shape
        outs = pl.pallas_call(
            functools.partial(gather_kernel, ntop, len(arrays), at[:nblk * ntop], at[nblk * ntop:]),
            out_shape=[jax.ShapeDtypeStruct((3 * nblk * pts, nc), jnp.bfloat16)] * ntop
            + [jax.ShapeDtypeStruct((nblk, nv, pts), jnp.float32)] * 2,
            in_specs=[SMEM] + [VMEM] * len(arrays),
            out_specs=[VMEM] * (ntop + 2),
            compiler_params=PARAMS,
            cost_estimate=COST,
        )(core.astype(jnp.int32)[None], *arrays)
        return after, outs[ntop:], outs[:ntop]
    tiles = [array[index] for array, index in tiles]
    rows = jnp.stack(tiles[nblk * ntop:]).reshape(nblk, 2, nv, -1)
    vals = [jnp.where(core == k, rows[:, 0], rows[:, 1]) for k in range(2)]
    return after, vals, [jnp.stack(tiles[a * nblk:(a + 1) * nblk]) for a in range(ntop)]


def apply_kernel(nchip, pair_ref, *refs):
    pots, (val_ref, right, out_ref, left) = refs[:nchip], refs[nchip:]
    nb, nv, nc = out_ref.shape
    pts = val_ref.shape[2]
    pair = pair_ref[0]
    for j in range(nchip):
        both = pots[j][...]
        for e in range(2):
            g = e * nchip + j
            pot = jnp.where((pair ^ e) == 0, both[:nb], both[nb:])
            rows = val_ref[g]
            for b in range(nb):
                high, low = split(rows * pot[b:b + 1])
                at = pl.ds(b * nv, nv)
                left[at, pl.ds(3 * g * pts, pts)] = high
                left[at, pl.ds((3 * g + 1) * pts, pts)] = high
                left[at, pl.ds((3 * g + 2) * pts, pts)] = low
    total = jnp.dot(left[...], right[...], preferred_element_type=jnp.float32)
    out_ref[...] = total.reshape(nb, nv, nc)


def applied(aligned, pair, pots, val, con, shape):
    nb, nv, nc = shape
    nblk = val.shape[0]
    nchip = nblk // 2
    pts = pots[0].shape[1]
    if aligned:
        return pl.pallas_call(
            functools.partial(apply_kernel, nchip),
            out_shape=jax.ShapeDtypeStruct(shape, jnp.float32),
            in_specs=[SMEM] + [VMEM] * (nchip + 2),
            out_specs=VMEM,
            scratch_shapes=[pltpu.VMEM((nb * nv, 3 * nblk * pts), jnp.bfloat16)],
            compiler_params=PARAMS,
            cost_estimate=COST,
        )(pair.astype(jnp.int32)[None], *pots, val, con)
    pot = relative(jnp.stack(pots).reshape(nchip, 2, nb, pts), 1, pair)
    pot = jnp.transpose(pot, (1, 0, 2, 3)).reshape(nblk, nb, pts)
    return jnp.einsum("gvp,gbp,gpc->bvc", val.reshape(nblk, nv, pts), pot, con.reshape(nblk, pts, nc), precision=HIGH)


def make(nchip, ntop):
    def rc_swap(x, mask):
        return swap(x, "rc", nchip, mask)

    def top_swap(x, mask):
        return swap(x, "top", ntop, mask)

    def pair_swap(x):
        return swap(x, "pair", 2, 1)

    def core_swap(x):
        return swap(x, "core", 2, 1)

    def col_swap(x, mask):
        n = 2 * ntop
        return lax.ppermute(x, ("top", "pair"), [(i, i ^ mask) for i in range(n)])

    def relay(tiles, j):
        high = 1 << (j.bit_length() - 1)
        low = j & -j
        out = []
        for a in range(ntop):
            mask = low if a % 2 else high
            array, index = tiles[j ^ mask][a]
            out.append((rc_swap(array[index:index + 1], mask), 0))
        return out

    def per_device(x_pairs, eps_val, eps_con, orb_val, orb_con, screened_w):
        rc = lax.axis_index("rc")
        core = lax.axis_index("core")
        top = lax.axis_index("top")
        pair = lax.axis_index("pair")
        nb, nv, nc = x_pairs.shape
        pts = orb_val.shape[0]
        aligned = nc % 128 == 0 and pts == nc and 2 * nv == nc

        packed = pack(nchip, ntop, aligned, rc, top, pair, orb_con, orb_val, nc)
        from_pair = pair_swap(packed[0])
        from_chip = {j: rc_swap(packed[j], j) for j in range(1, nchip)}
        x_tops = [x_pairs] + [top_swap(x_pairs, a) for a in range(1, ntop)]
        x_tops, from_pair, from_chip = lax.optimization_barrier((x_tops, from_pair, from_chip))

        val = [{0: (packed[-1], 0)}, {}]
        con = [{0: [(packed[1], a) for a in range(ntop)]}, {0: [(from_pair, a) for a in range(ntop)]}]
        singles = [j for j in range(1, nchip) if single(j)]
        others = [j for j in range(1, nchip) if not single(j)]
        for j in range(1, nchip):
            val[0][j] = (from_chip[j], from_chip[j].shape[0] - 1)
            if single(j):
                con[0][j] = [(from_chip[j], a) for a in range(ntop)]

        def pair_val(part):
            got = pair_swap(jnp.stack([val[0][j][0][val[0][j][1]] for j in part]))
            for i, j in enumerate(part):
                val[1][j] = (got, i)

        pair_val([0] + singles)
        if nchip == 4:
            con[0][3] = [None] * ntop
            for mask in (2, 1):
                mine = [a for a in range(ntop) if (a % 2 == 0) == (mask == 2)]
                tiles = [con[0][3 ^ mask][a] for a in mine] + con[1][0]
                got = rc_swap(jnp.stack([array[index] for array, index in tiles]), mask)
                for i, a in enumerate(mine):
                    con[0][3][a] = (got, i)
                con[1][mask] = [(got, len(mine) + a) for a in range(ntop)]
        else:
            for j in others:
                con[0][j] = relay(con[0], j)
            for j in singles:
                got = rc_swap(from_pair, j)
                con[1][j] = [(got, a) for a in range(ntop)]

        x = [[t, core_swap(t)] for t in x_tops]
        if aligned:
            x = halves(x)
        else:
            x = [jnp.where(core == 0, jnp.stack(row, 1), jnp.stack(row[::-1], 1)) for row in x]

        def density(group):
            return densities(
                aligned, core, x_pairs.shape, x, [con[e][j] for e, j in group], [val[e][j] for e, j in group]
            )

        groups = [[(0, 0)] + [(0, j) for j in singles]]
        dens = [density(groups[0])]
        if others:
            arrays = [con[1][j][0][0] for j in singles] + [val[0][j][0] for j in others]
            dens[0], arrays = ordered(dens[0], arrays)
            con[1].update({j: [(arrays[i], index) for _, index in con[1][j]] for i, j in enumerate(singles)})
            for i, j in enumerate(others):
                val[0][j] = (arrays[len(singles) + i], val[0][j][1])
            for j in others:
                con[1][j] = relay(con[1], j)
            pair_val(others)
        groups += [
            [(0, j) for j in others],
            [(1, 0)] + [(1, j) for j in singles],
            [(1, j) for j in others],
        ]
        groups = [group for group in groups if group]
        dens += [density(group) for group in groups[1:]]
        order = [e * nchip + j for group in groups for e, j in group]
        part = route(aligned, nchip, rc, pair, order, dens)
        got = lax.all_to_all(part, ("rc", "core", "top", "pair"), 0, 0, tiled=True)
        rows = screen(aligned, nchip, ntop, top, got, screened_w)
        vals = [val[e][j] for e in range(2) for j in range(nchip)]
        cons = [[con[e][j][a] for e in range(2) for j in range(nchip)] for a in range(ntop)]
        rows = list(rows)
        rows[0], vals, cons = gathered(aligned, core, rows[0], vals, cons, nv)
        row = rows[0]
        for d in range(1, 2 * ntop):
            row = row + col_swap(rows[d // 2], d)
        pots = [row] + [rc_swap(row, j) for j in range(1, nchip)]

        def apply(a, k):
            return applied(aligned, pair, pots, vals[k], cons[a], x_pairs.shape)

        base = (eps_con[None, None, :] - eps_val[None, :, None]) * x_pairs
        for a in list(range(1, ntop)) + [0]:
            away, step = apply(a, 1), apply(a, 0)
            if a:
                step, pots[0] = lax.optimization_barrier((step + core_swap(away), pots[0]))
                base = base + top_swap(step, a)
        return lax.optimization_barrier(base) + step + core_swap(away)

    return per_device


def solution(mesh):
    nrow, ncol = mesh.shape["rowpt"], mesh.shape["colpt"]
    nchip, ntop = nrow // 2, ncol // 2
    fine = Mesh(mesh.devices.reshape(nchip, 2, ntop, 2), ("rc", "core", "top", "pair"))
    row, col = ("rc", "core"), ("top", "pair")
    in_specs = (P(None, row, col), P(row), P(col), P(row + col, None), P(row + col, None), P(row, col))
    return jax.shard_map(
        make(nchip, ntop), mesh=fine, in_specs=in_specs, out_specs=P(None, row, col), check_vma=False
    )
```

```python
import functools

import jax
import jax.numpy as jnp
from jax import lax
from jax.experimental import pallas as pl
from jax.experimental.pallas import tpu as pltpu
from jax.sharding import Mesh, PartitionSpec as P

HIGH = lax.Precision.HIGH
VMEM = pl.BlockSpec(memory_space=pltpu.VMEM)
ANY = pl.BlockSpec(memory_space=pl.ANY)
SMEM = pl.BlockSpec(memory_space=pltpu.SMEM)
COST = pl.CostEstimate(flops=2 * 10**9, bytes_accessed=4 * 2**20, transcendentals=0)
PARAMS = pltpu.CompilerParams(vmem_limit_bytes=14 * 1024 * 1024)


def swap(x, axis, size, mask):
    return lax.ppermute(x, axis, [(i, i ^ mask) for i in range(size)])


def relative(x, axis, index):
    size = x.shape[axis]
    bit = 1
    while bit < size:
        shape = x.shape[:axis] + (size // (2 * bit), 2, bit) + x.shape[axis + 1:]
        flipped = jnp.flip(x.reshape(shape), axis + 1).reshape(x.shape)
        x = jnp.where((index & bit) != 0, flipped, x)
        bit *= 2
    return x


def ordered(first, then):
    return lax.optimization_barrier((first, then))


def single(j):
    return j & (j - 1) == 0


def split(x):
    high = x.astype(jnp.bfloat16)
    return high, (x - high.astype(jnp.float32)).astype(jnp.bfloat16)


def pack_kernel(nchip, ntop, where, con_ref, val_ref, *outs):
    nc = outs[0].shape[2]
    rc, top, pair = where[0], where[1], where[2]

    def con_tile(a, e):
        at = ((top ^ a) * 2 + (pair ^ e)) * nc
        return con_ref[:, pl.ds(pl.multiple_of(at, nc), nc)]

    def val_tile(j):
        at = (rc ^ j) * nc
        return val_ref[:, pl.ds(pl.multiple_of(at, nc), nc)].T

    for j in range(nchip + 1):
        out = outs[j]
        if j == 0 or (j < nchip and single(j)):
            for a in range(ntop):
                out[a] = con_tile(a, int(j == 0))
        if j:
            out[out.shape[0] - 1] = val_tile(j % nchip)


def pack(nchip, ntop, aligned, rc, top, pair, orb_con, orb_val, nc):
    pts = orb_con.shape[0]
    if aligned:
        sizes = [ntop] + [ntop + 1 if single(j) else 1 for j in range(1, nchip)] + [1]
        return pl.pallas_call(
            functools.partial(pack_kernel, nchip, ntop),
            out_shape=[jax.ShapeDtypeStruct((s, pts, nc), jnp.float32) for s in sizes],
            in_specs=[SMEM, VMEM, VMEM],
            out_specs=[VMEM] * (nchip + 1),
            compiler_params=PARAMS,
            cost_estimate=COST,
        )(jnp.stack([rc, top, pair]).astype(jnp.int32), orb_con, orb_val)

    def con_tile(a, e):
        return lax.dynamic_slice_in_dim(orb_con, ((top ^ a) * 2 + (pair ^ e)) * nc, nc, 1)

    def val_tile(j):
        return lax.dynamic_slice_in_dim(orb_val, (rc ^ j) * nc, nc, 1).T.reshape(pts, nc)

    out = [jnp.stack([con_tile(a, 1) for a in range(ntop)])]
    for j in range(1, nchip):
        con = [con_tile(a, 0) for a in range(ntop)] if single(j) else []
        out.append(jnp.stack(con + [val_tile(j)]))
    return out + [val_tile(0)[None]]


def operands(tiles):
    arrays, at = [], []
    for array, index in tiles:
        where = [i for i, other in enumerate(arrays) if other is array]
        if not where:
            arrays.append(array)
            where = [len(arrays) - 1]
        at.append((where[0], index))
    return arrays, at


def halves_kernel(x_refs, out_ref):
    nb, nv, nc = x_refs[0].shape
    width = out_ref.shape[1] // 2
    for i, ref in enumerate(x_refs):
        a, k = i // 2, i % 2
        high, low = split(ref[...].reshape(nb * nv, nc))
        rows = pl.ds(k * nb * nv, nb * nv)
        out_ref[rows, pl.ds(a * nc, nc)] = high
        out_ref[rows, pl.ds(width + a * nc, nc)] = low


def halves(x):
    flat = [t for row in x for t in row]
    nb, nv, nc = flat[0].shape
    return pl.pallas_call(
        lambda *refs: halves_kernel(refs[:-1], refs[-1]),
        out_shape=jax.ShapeDtypeStruct((2 * nb * nv, 2 * len(x) * nc), jnp.bfloat16),
        in_specs=[VMEM] * len(flat),
        out_specs=VMEM,
        compiler_params=PARAMS,
        cost_estimate=COST,
    )(*flat)


def density_kernel(nblk, ntop, shape, con_at, val_at, core_ref, x_ref, *refs):
    tiles, (dens_ref, right) = refs[:-2], refs[-2:]
    nb, nv, nc = shape
    width = ntop * nc
    core = core_ref[0]
    for g in range(nblk):
        for a in range(ntop):
            array, index = con_at[g * ntop + a]
            high, low = split(tiles[array][index])
            right[g, :, pl.ds(a * nc, nc)] = high
            right[g, :, pl.ds(width + a * nc, nc)] = high
            right[g, :, pl.ds(2 * width + a * nc, nc)] = low
        array, index = val_at[g]
        total = None
        for k in range(2):
            at = pl.ds(k * nb * nv, nb * nv)
            left = jnp.concatenate([x_ref[at, :], x_ref[at, pl.ds(0, width)]], axis=1)
            through = lax.dot_general(
                left, right[g], (((1,), (1,)), ((), ())), preferred_element_type=jnp.float32
            )
            rows = tiles[array][index, pl.ds(pl.multiple_of((core ^ k) * nv, nv), nv), :]
            part = jnp.sum(through.reshape(nb, nv, -1) * rows[None], axis=1)
            total = part if total is None else total + part
        dens_ref[g] = total


def densities(aligned, core, shape, x, con, val):
    nblk, ntop = len(con), len(con[0])
    nb, nv, nc = shape
    if aligned:
        arrays, at = operands([t for row in con for t in row] + list(val))
        pts = arrays[0].shape[1]
        return pl.pallas_call(
            functools.partial(density_kernel, nblk, ntop, shape, at[:nblk * ntop], at[nblk * ntop:]),
            out_shape=jax.ShapeDtypeStruct((nblk, nb, pts), jnp.float32),
            in_specs=[SMEM] + [VMEM] * (1 + len(arrays)),
            out_specs=VMEM,
            scratch_shapes=[pltpu.VMEM((nblk, pts, 3 * ntop * nc), jnp.bfloat16)],
            compiler_params=PARAMS,
            cost_estimate=COST,
        )(core.astype(jnp.int32)[None], x, *arrays)
    out = []
    for g in range(nblk):
        through = 0.0
        for a in range(ntop):
            array, index = con[g][a]
            through = through + jnp.einsum("bkvc,pc->bkvp", x[a], array[index], precision=HIGH)
        array, index = val[g]
        out.append(jnp.sum(through * array[index].reshape(1, 2, nv, -1), axis=(1, 2)))
    return jnp.stack(out)


def route_kernel(order, nchip, where, *refs):
    groups, out_ref, held = refs[:-2], refs[-2], refs[-1]
    nb = held.shape[1]
    rc, pair = where[0], where[1]
    at = 0
    for ref in groups:
        for g in range(ref.shape[0]):
            held[order[at]] = ref[g]
            at += 1
    for z in range(nchip):
        for p in range(2):
            piece = held[(pair ^ p) * nchip + (rc ^ z)]
            for d in range(out_ref.shape[0] // nchip):
                out_ref[d * nchip + z, pl.ds(p * nb, nb), :] = piece


def route(aligned, nchip, rc, pair, order, groups):
    nb, pts = groups[0].shape[1:]
    if aligned:
        return pl.pallas_call(
            functools.partial(route_kernel, order, nchip),
            out_shape=jax.ShapeDtypeStruct((2 * nchip * nchip, 2 * nb, pts), jnp.float32),
            in_specs=[SMEM] + [VMEM] * len(groups),
            out_specs=VMEM,
            scratch_shapes=[pltpu.VMEM((2 * nchip, nb, pts), jnp.float32)],
            compiler_params=PARAMS,
            cost_estimate=COST,
        )(jnp.stack([rc, pair]).astype(jnp.int32), *groups)
    flat = jnp.concatenate(groups)
    flat = jnp.stack([flat[order.index(i)] for i in range(2 * nchip)]).reshape(2, nchip, nb, pts)
    flat = jnp.transpose(relative(relative(flat, 1, rc), 0, pair), (1, 0, 2, 3)).reshape(nchip, 2 * nb, pts)
    return jnp.tile(flat, (2 * nchip, 1, 1))


def screen_kernel(nchip, ntop, top_ref, got_ref, w_ref, *refs):
    outs, (dens, left) = refs[:ntop], refs[ntop:]
    nb = got_ref.shape[1] // 2
    pts = got_ref.shape[2]
    top = top_ref[0]
    for k in range(2):
        for t in range(ntop):
            total = None
            for r in range(nchip):
                for p in range(2):
                    piece = got_ref[((r * 2 + k) * ntop + t) * 2 + p]
                    total = piece if total is None else total + piece
            for p in range(2):
                dens[:, pl.ds(((k * ntop + t) * 2 + p) * pts, pts)] = total[p * nb:(p + 1) * nb]
    high, low = split(dens[...])
    left[...] = jnp.zeros_like(left)
    left[pl.ds(0, nb), :] = high
    left[pl.ds(nb, nb), :] = low
    for a in range(ntop):
        for p in range(2):
            at = pl.multiple_of(((top ^ a) * 2 + p) * pts, pts)
            high, low = split(w_ref[pl.ds(at, pts), :])
            dims = (((1,), (1,)), ((), ()))
            total = lax.dot_general(left[...], high, dims, preferred_element_type=jnp.float32)
            extra = lax.dot_general(left[...], low, dims, preferred_element_type=jnp.float32)
            outs[a][pl.ds(p * nb, nb), :] = total[:nb] + total[nb:2 * nb] + extra[:nb]


def screen(aligned, nchip, ntop, top, got, screened_w):
    nb, pts = got.shape[1] // 2, got.shape[2]
    if aligned:
        nq = screened_w.shape[1]
        return pl.pallas_call(
            functools.partial(screen_kernel, nchip, ntop),
            out_shape=[jax.ShapeDtypeStruct((2 * nb, pts), jnp.float32)] * ntop,
            in_specs=[SMEM, VMEM, VMEM],
            out_specs=[VMEM] * ntop,
            scratch_shapes=[pltpu.VMEM((nb, nq), jnp.float32), pltpu.VMEM((16, nq), jnp.bfloat16)],
            compiler_params=PARAMS,
            cost_estimate=COST,
        )(top.astype(jnp.int32)[None], got, screened_w)
    density = jnp.sum(got.reshape(nchip, 2, ntop, 2, 2, nb, pts), axis=(0, 3))
    density = jnp.transpose(density.reshape(-1, nb, pts), (1, 0, 2)).reshape(nb, -1)
    rows = lax.dot_general(density, screened_w, (((1,), (1,)), ((), ())), precision=HIGH)
    rows = jnp.transpose(rows.reshape(nb, ntop, 2, pts), (1, 2, 0, 3)).reshape(ntop, 2 * nb, pts)
    rows = relative(rows, 0, top)
    return [rows[a] for a in range(ntop)]


def gather_kernel(ntop, nin, con_at, val_at, core_ref, *refs):
    tiles, rights, val_refs = refs[:nin], refs[nin:nin + ntop], refs[nin + ntop:]
    nblk, nv, pts = val_refs[0].shape
    core = core_ref[0]
    for g in range(nblk):
        for a in range(ntop):
            array, index = con_at[a * nblk + g]
            high, low = split(tiles[array][index])
            rights[a][pl.ds(3 * g * pts, pts), :] = high
            rights[a][pl.ds((3 * g + 1) * pts, pts), :] = low
            rights[a][pl.ds((3 * g + 2) * pts, pts), :] = high
        array, index = val_at[g]
        for k in range(2):
            val_refs[k][g] = tiles[array][index, pl.ds(pl.multiple_of((core ^ k) * nv, nv), nv), :]


def gathered(aligned, core, after, val, con, nv):
    nblk, ntop = len(val), len(con)
    arrays, at = operands([t for row in con for t in row] + val)
    after, *arrays = lax.optimization_barrier((after, *arrays))
    tiles = [(arrays[i], index) for i, index in at]
    if aligned:
        _, pts, nc = arrays[0].shape
        outs = pl.pallas_call(
            functools.partial(gather_kernel, ntop, len(arrays), at[:nblk * ntop], at[nblk * ntop:]),
            out_shape=[jax.ShapeDtypeStruct((3 * nblk * pts, nc), jnp.bfloat16)] * ntop
            + [jax.ShapeDtypeStruct((nblk, nv, pts), jnp.float32)] * 2,
            in_specs=[SMEM] + [VMEM] * len(arrays),
            out_specs=[VMEM] * (ntop + 2),
            compiler_params=PARAMS,
            cost_estimate=COST,
        )(core.astype(jnp.int32)[None], *arrays)
        return after, outs[ntop:], outs[:ntop]
    tiles = [array[index] for array, index in tiles]
    rows = jnp.stack(tiles[nblk * ntop:]).reshape(nblk, 2, nv, -1)
    vals = [jnp.where(core == k, rows[:, 0], rows[:, 1]) for k in range(2)]
    return after, vals, [jnp.stack(tiles[a * nblk:(a + 1) * nblk]) for a in range(ntop)]


def apply_kernel(nchip, pair_ref, *refs):
    pots, (val_ref, right, out_ref, left) = refs[:nchip], refs[nchip:]
    nb, nv, nc = out_ref.shape
    pts = val_ref.shape[2]
    pair = pair_ref[0]
    for j in range(nchip):
        both = pots[j][...]
        for e in range(2):
            g = e * nchip + j
            pot = jnp.where((pair ^ e) == 0, both[:nb], both[nb:])
            rows = val_ref[g]
            for b in range(nb):
                high, low = split(rows * pot[b:b + 1])
                at = pl.ds(b * nv, nv)
                left[at, pl.ds(3 * g * pts, pts)] = high
                left[at, pl.ds((3 * g + 1) * pts, pts)] = high
                left[at, pl.ds((3 * g + 2) * pts, pts)] = low
    total = jnp.dot(left[...], right[...], preferred_element_type=jnp.float32)
    out_ref[...] = total.reshape(nb, nv, nc)


def applied(aligned, pair, pots, val, con, shape):
    nb, nv, nc = shape
    nblk = val.shape[0]
    nchip = nblk // 2
    pts = pots[0].shape[1]
    if aligned:
        return pl.pallas_call(
            functools.partial(apply_kernel, nchip),
            out_shape=jax.ShapeDtypeStruct(shape, jnp.float32),
            in_specs=[SMEM] + [VMEM] * (nchip + 2),
            out_specs=VMEM,
            scratch_shapes=[pltpu.VMEM((nb * nv, 3 * nblk * pts), jnp.bfloat16)],
            compiler_params=PARAMS,
            cost_estimate=COST,
        )(pair.astype(jnp.int32)[None], *pots, val, con)
    pot = relative(jnp.stack(pots).reshape(nchip, 2, nb, pts), 1, pair)
    pot = jnp.transpose(pot, (1, 0, 2, 3)).reshape(nblk, nb, pts)
    return jnp.einsum("gvp,gbp,gpc->bvc", val.reshape(nblk, nv, pts), pot, con.reshape(nblk, pts, nc), precision=HIGH)


def make(nchip, ntop):
    def rc_swap(x, mask):
        return swap(x, "rc", nchip, mask)

    def top_swap(x, mask):
        return swap(x, "top", ntop, mask)

    def pair_swap(x):
        return swap(x, "pair", 2, 1)

    def core_swap(x):
        return swap(x, "core", 2, 1)

    def col_swap(x, mask):
        n = 2 * ntop
        return lax.ppermute(x, ("top", "pair"), [(i, i ^ mask) for i in range(n)])

    def relay(tiles, j):
        high = 1 << (j.bit_length() - 1)
        low = j & -j
        out = []
        for a in range(ntop):
            mask = low if a % 2 else high
            array, index = tiles[j ^ mask][a]
            out.append((rc_swap(array[index:index + 1], mask), 0))
        return out

    def per_device(x_pairs, eps_val, eps_con, orb_val, orb_con, screened_w):
        rc = lax.axis_index("rc")
        core = lax.axis_index("core")
        top = lax.axis_index("top")
        pair = lax.axis_index("pair")
        nb, nv, nc = x_pairs.shape
        pts = orb_val.shape[0]
        aligned = nc % 128 == 0 and pts == nc and 2 * nv == nc

        packed = pack(nchip, ntop, aligned, rc, top, pair, orb_con, orb_val, nc)
        from_pair = pair_swap(packed[0])
        from_chip = {j: rc_swap(packed[j], j) for j in range(1, nchip)}
        x_tops = [x_pairs] + [top_swap(x_pairs, a) for a in range(1, ntop)]
        from_pair, from_chip = lax.optimization_barrier((from_pair, from_chip))

        val = [{0: (packed[-1], 0)}, {}]
        con = [{0: [(packed[1], a) for a in range(ntop)]}, {0: [(from_pair, a) for a in range(ntop)]}]
        singles = [j for j in range(1, nchip) if single(j)]
        others = [j for j in range(1, nchip) if not single(j)]
        for j in range(1, nchip):
            val[0][j] = (from_chip[j], from_chip[j].shape[0] - 1)
            if single(j):
                con[0][j] = [(from_chip[j], a) for a in range(ntop)]

        def pair_val(part):
            got = pair_swap(jnp.stack([val[0][j][0][val[0][j][1]] for j in part]))
            for i, j in enumerate(part):
                val[1][j] = (got, i)

        pair_val([0] + singles)
        for j in singles:
            got = rc_swap(from_pair, j)
            con[1][j] = [(got, a) for a in range(ntop)]
        for j in others:
            con[0][j] = relay(con[0], j)

        x = [[t, core_swap(t)] for t in x_tops]
        if aligned:
            x = halves(x)
        else:
            x = [jnp.where(core == 0, jnp.stack(row, 1), jnp.stack(row[::-1], 1)) for row in x]

        def density(group):
            return densities(
                aligned, core, x_pairs.shape, x, [con[e][j] for e, j in group], [val[e][j] for e, j in group]
            )

        groups = [[(0, 0)] + [(0, j) for j in singles]]
        dens = [density(groups[0])]
        if others:
            arrays = [con[1][j][0][0] for j in singles] + [val[0][j][0] for j in others]
            dens[0], arrays = ordered(dens[0], arrays)
            con[1].update({j: [(arrays[i], index) for _, index in con[1][j]] for i, j in enumerate(singles)})
            for i, j in enumerate(others):
                val[0][j] = (arrays[len(singles) + i], val[0][j][1])
            for j in others:
                con[1][j] = relay(con[1], j)
            pair_val(others)
        groups += [
            [(0, j) for j in others],
            [(1, 0)] + [(1, j) for j in singles],
            [(1, j) for j in others],
        ]
        groups = [group for group in groups if group]
        dens += [density(group) for group in groups[1:]]
        order = [e * nchip + j for group in groups for e, j in group]
        part = route(aligned, nchip, rc, pair, order, dens)
        got = lax.all_to_all(part, ("rc", "core", "top", "pair"), 0, 0, tiled=True)
        rows = screen(aligned, nchip, ntop, top, got, screened_w)
        vals = [val[e][j] for e in range(2) for j in range(nchip)]
        cons = [[con[e][j][a] for e in range(2) for j in range(nchip)] for a in range(ntop)]
        rows = list(rows)
        rows[0], vals, cons = gathered(aligned, core, rows[0], vals, cons, nv)
        row = rows[0]
        for d in range(1, 2 * ntop):
            row = row + col_swap(rows[d // 2], d)
        pots = [row] + [rc_swap(row, j) for j in range(1, nchip)]

        def apply(a, k):
            return applied(aligned, pair, pots, vals[k], cons[a], x_pairs.shape)

        base = (eps_con[None, None, :] - eps_val[None, :, None]) * x_pairs
        sent = None
        for a in list(range(1, ntop)) + [0]:
            away, step = apply(a, 1), apply(a, 0)
            if a:
                step, pots[0] = lax.optimization_barrier((step + core_swap(away), pots[0]))
                piece = top_swap(step, a)
                sent = piece if sent is None else sent + piece
            else:
                size = nb // 4
                parts = [core_swap(away[i * size:(i + 1) * size]) for i in range(4)]
                base = lax.optimization_barrier(base + step + jnp.concatenate(parts, axis=0))
        return base if sent is None else base + sent

    return per_device


def solution(mesh):
    nrow, ncol = mesh.shape["rowpt"], mesh.shape["colpt"]
    nchip, ntop = nrow // 2, ncol // 2
    fine = Mesh(mesh.devices.reshape(nchip, 2, ntop, 2), ("rc", "core", "top", "pair"))
    row, col = ("rc", "core"), ("top", "pair")
    in_specs = (P(None, row, col), P(row), P(col), P(row + col, None), P(row + col, None), P(row, col))
    return jax.shard_map(
        make(nchip, ntop), mesh=fine, in_specs=in_specs, out_specs=P(None, row, col), check_vma=False
    )
```

```python
import functools

import jax
import jax.numpy as jnp
from jax import lax
from jax.experimental import pallas as pl
from jax.experimental.pallas import tpu as pltpu
from jax.sharding import Mesh, PartitionSpec as P

HIGH = lax.Precision.HIGH
VMEM = pl.BlockSpec(memory_space=pltpu.VMEM)
ANY = pl.BlockSpec(memory_space=pl.ANY)
SMEM = pl.BlockSpec(memory_space=pltpu.SMEM)
COST = pl.CostEstimate(flops=2 * 10**9, bytes_accessed=4 * 2**20, transcendentals=0)
PARAMS = pltpu.CompilerParams(vmem_limit_bytes=14 * 1024 * 1024)


def swap(x, axis, size, mask):
    return lax.ppermute(x, axis, [(i, i ^ mask) for i in range(size)])


def relative(x, axis, index):
    size = x.shape[axis]
    bit = 1
    while bit < size:
        shape = x.shape[:axis] + (size // (2 * bit), 2, bit) + x.shape[axis + 1:]
        flipped = jnp.flip(x.reshape(shape), axis + 1).reshape(x.shape)
        x = jnp.where((index & bit) != 0, flipped, x)
        bit *= 2
    return x


def ordered(first, then):
    return lax.optimization_barrier((first, then))


def single(j):
    return j & (j - 1) == 0


def split(x):
    high = x.astype(jnp.bfloat16)
    return high, (x - high.astype(jnp.float32)).astype(jnp.bfloat16)


def pack_kernel(nchip, ntop, where, con_ref, val_ref, *outs):
    nc = outs[0].shape[2]
    rc, top, pair = where[0], where[1], where[2]

    def con_tile(a, e):
        at = ((top ^ a) * 2 + (pair ^ e)) * nc
        return con_ref[:, pl.ds(pl.multiple_of(at, nc), nc)]

    def val_tile(j):
        at = (rc ^ j) * nc
        return val_ref[:, pl.ds(pl.multiple_of(at, nc), nc)].T

    for j in range(nchip + 1):
        out = outs[j]
        if j == 0 or (j < nchip and single(j)):
            for a in range(ntop):
                out[a] = con_tile(a, int(j == 0))
        if j:
            out[out.shape[0] - 1] = val_tile(j % nchip)


def pack(nchip, ntop, aligned, rc, top, pair, orb_con, orb_val, nc):
    pts = orb_con.shape[0]
    if aligned:
        sizes = [ntop] + [ntop + 1 if single(j) else 1 for j in range(1, nchip)] + [1]
        return pl.pallas_call(
            functools.partial(pack_kernel, nchip, ntop),
            out_shape=[jax.ShapeDtypeStruct((s, pts, nc), jnp.float32) for s in sizes],
            in_specs=[SMEM, VMEM, VMEM],
            out_specs=[VMEM] * (nchip + 1),
            compiler_params=PARAMS,
            cost_estimate=COST,
        )(jnp.stack([rc, top, pair]).astype(jnp.int32), orb_con, orb_val)

    def con_tile(a, e):
        return lax.dynamic_slice_in_dim(orb_con, ((top ^ a) * 2 + (pair ^ e)) * nc, nc, 1)

    def val_tile(j):
        return lax.dynamic_slice_in_dim(orb_val, (rc ^ j) * nc, nc, 1).T.reshape(pts, nc)

    out = [jnp.stack([con_tile(a, 1) for a in range(ntop)])]
    for j in range(1, nchip):
        con = [con_tile(a, 0) for a in range(ntop)] if single(j) else []
        out.append(jnp.stack(con + [val_tile(j)]))
    return out + [val_tile(0)[None]]


def operands(tiles):
    arrays, at = [], []
    for array, index in tiles:
        where = [i for i, other in enumerate(arrays) if other is array]
        if not where:
            arrays.append(array)
            where = [len(arrays) - 1]
        at.append((where[0], index))
    return arrays, at


def halves_kernel(x_refs, out_ref):
    nb, nv, nc = x_refs[0].shape
    width = out_ref.shape[1] // 2
    for i, ref in enumerate(x_refs):
        a, k = i // 2, i % 2
        high, low = split(ref[...].reshape(nb * nv, nc))
        rows = pl.ds(k * nb * nv, nb * nv)
        out_ref[rows, pl.ds(a * nc, nc)] = high
        out_ref[rows, pl.ds(width + a * nc, nc)] = low


def halves(x):
    flat = [t for row in x for t in row]
    nb, nv, nc = flat[0].shape
    return pl.pallas_call(
        lambda *refs: halves_kernel(refs[:-1], refs[-1]),
        out_shape=jax.ShapeDtypeStruct((2 * nb * nv, 2 * len(x) * nc), jnp.bfloat16),
        in_specs=[VMEM] * len(flat),
        out_specs=VMEM,
        compiler_params=PARAMS,
        cost_estimate=COST,
    )(*flat)


def density_kernel(nblk, ntop, shape, con_at, val_at, core_ref, x_ref, *refs):
    tiles, (dens_ref, right) = refs[:-2], refs[-2:]
    nb, nv, nc = shape
    width = ntop * nc
    core = core_ref[0]
    for g in range(nblk):
        for a in range(ntop):
            array, index = con_at[g * ntop + a]
            high, low = split(tiles[array][index])
            right[g, :, pl.ds(a * nc, nc)] = high
            right[g, :, pl.ds(width + a * nc, nc)] = high
            right[g, :, pl.ds(2 * width + a * nc, nc)] = low
        array, index = val_at[g]
        total = None
        for k in range(2):
            at = pl.ds(k * nb * nv, nb * nv)
            left = jnp.concatenate([x_ref[at, :], x_ref[at, pl.ds(0, width)]], axis=1)
            through = lax.dot_general(
                left, right[g], (((1,), (1,)), ((), ())), preferred_element_type=jnp.float32
            )
            rows = tiles[array][index, pl.ds(pl.multiple_of((core ^ k) * nv, nv), nv), :]
            part = jnp.sum(through.reshape(nb, nv, -1) * rows[None], axis=1)
            total = part if total is None else total + part
        dens_ref[g] = total


def densities(aligned, core, shape, x, con, val):
    nblk, ntop = len(con), len(con[0])
    nb, nv, nc = shape
    if aligned:
        arrays, at = operands([t for row in con for t in row] + list(val))
        pts = arrays[0].shape[1]
        return pl.pallas_call(
            functools.partial(density_kernel, nblk, ntop, shape, at[:nblk * ntop], at[nblk * ntop:]),
            out_shape=jax.ShapeDtypeStruct((nblk, nb, pts), jnp.float32),
            in_specs=[SMEM] + [VMEM] * (1 + len(arrays)),
            out_specs=VMEM,
            scratch_shapes=[pltpu.VMEM((nblk, pts, 3 * ntop * nc), jnp.bfloat16)],
            compiler_params=PARAMS,
            cost_estimate=COST,
        )(core.astype(jnp.int32)[None], x, *arrays)
    out = []
    for g in range(nblk):
        through = 0.0
        for a in range(ntop):
            array, index = con[g][a]
            through = through + jnp.einsum("bkvc,pc->bkvp", x[a], array[index], precision=HIGH)
        array, index = val[g]
        out.append(jnp.sum(through * array[index].reshape(1, 2, nv, -1), axis=(1, 2)))
    return jnp.stack(out)


def route_kernel(order, nchip, where, *refs):
    groups, out_ref, held = refs[:-2], refs[-2], refs[-1]
    nb = held.shape[1]
    rc, pair = where[0], where[1]
    at = 0
    for ref in groups:
        for g in range(ref.shape[0]):
            held[order[at]] = ref[g]
            at += 1
    for z in range(nchip):
        for p in range(2):
            piece = held[(pair ^ p) * nchip + (rc ^ z)]
            for d in range(out_ref.shape[0] // nchip):
                out_ref[d * nchip + z, pl.ds(p * nb, nb), :] = piece


def route(aligned, nchip, rc, pair, order, groups):
    nb, pts = groups[0].shape[1:]
    if aligned:
        return pl.pallas_call(
            functools.partial(route_kernel, order, nchip),
            out_shape=jax.ShapeDtypeStruct((2 * nchip * nchip, 2 * nb, pts), jnp.float32),
            in_specs=[SMEM] + [VMEM] * len(groups),
            out_specs=VMEM,
            scratch_shapes=[pltpu.VMEM((2 * nchip, nb, pts), jnp.float32)],
            compiler_params=PARAMS,
            cost_estimate=COST,
        )(jnp.stack([rc, pair]).astype(jnp.int32), *groups)
    flat = jnp.concatenate(groups)
    flat = jnp.stack([flat[order.index(i)] for i in range(2 * nchip)]).reshape(2, nchip, nb, pts)
    flat = jnp.transpose(relative(relative(flat, 1, rc), 0, pair), (1, 0, 2, 3)).reshape(nchip, 2 * nb, pts)
    return jnp.tile(flat, (2 * nchip, 1, 1))


def screen_kernel(nchip, ntop, top_ref, got_ref, w_ref, *refs):
    outs, (dens, left) = refs[:ntop], refs[ntop:]
    nb = got_ref.shape[1] // 2
    pts = got_ref.shape[2]
    top = top_ref[0]
    for k in range(2):
        for t in range(ntop):
            total = None
            for r in range(nchip):
                for p in range(2):
                    piece = got_ref[((r * 2 + k) * ntop + t) * 2 + p]
                    total = piece if total is None else total + piece
            for p in range(2):
                dens[:, pl.ds(((k * ntop + t) * 2 + p) * pts, pts)] = total[p * nb:(p + 1) * nb]
    high, low = split(dens[...])
    left[...] = jnp.zeros_like(left)
    left[pl.ds(0, nb), :] = high
    left[pl.ds(nb, nb), :] = low
    for a in range(ntop):
        for p in range(2):
            at = pl.multiple_of(((top ^ a) * 2 + p) * pts, pts)
            high, low = split(w_ref[pl.ds(at, pts), :])
            dims = (((1,), (1,)), ((), ()))
            total = lax.dot_general(left[...], high, dims, preferred_element_type=jnp.float32)
            extra = lax.dot_general(left[...], low, dims, preferred_element_type=jnp.float32)
            outs[a][pl.ds(p * nb, nb), :] = total[:nb] + total[nb:2 * nb] + extra[:nb]


def screen(aligned, nchip, ntop, top, got, screened_w):
    nb, pts = got.shape[1] // 2, got.shape[2]
    if aligned:
        nq = screened_w.shape[1]
        return pl.pallas_call(
            functools.partial(screen_kernel, nchip, ntop),
            out_shape=[jax.ShapeDtypeStruct((2 * nb, pts), jnp.float32)] * ntop,
            in_specs=[SMEM, VMEM, VMEM],
            out_specs=[VMEM] * ntop,
            scratch_shapes=[pltpu.VMEM((nb, nq), jnp.float32), pltpu.VMEM((16, nq), jnp.bfloat16)],
            compiler_params=PARAMS,
            cost_estimate=COST,
        )(top.astype(jnp.int32)[None], got, screened_w)
    density = jnp.sum(got.reshape(nchip, 2, ntop, 2, 2, nb, pts), axis=(0, 3))
    density = jnp.transpose(density.reshape(-1, nb, pts), (1, 0, 2)).reshape(nb, -1)
    rows = lax.dot_general(density, screened_w, (((1,), (1,)), ((), ())), precision=HIGH)
    rows = jnp.transpose(rows.reshape(nb, ntop, 2, pts), (1, 2, 0, 3)).reshape(ntop, 2 * nb, pts)
    rows = relative(rows, 0, top)
    return [rows[a] for a in range(ntop)]


def gather_kernel(ntop, nin, con_at, val_at, core_ref, *refs):
    tiles, rights, val_refs = refs[:nin], refs[nin:nin + ntop], refs[nin + ntop:]
    nblk, nv, pts = val_refs[0].shape
    core = core_ref[0]
    for g in range(nblk):
        for a in range(ntop):
            array, index = con_at[a * nblk + g]
            high, low = split(tiles[array][index])
            rights[a][pl.ds(3 * g * pts, pts), :] = high
            rights[a][pl.ds((3 * g + 1) * pts, pts), :] = low
            rights[a][pl.ds((3 * g + 2) * pts, pts), :] = high
        array, index = val_at[g]
        for k in range(2):
            val_refs[k][g] = tiles[array][index, pl.ds(pl.multiple_of((core ^ k) * nv, nv), nv), :]


def gathered(aligned, core, after, val, con, nv):
    nblk, ntop = len(val), len(con)
    arrays, at = operands([t for row in con for t in row] + val)
    after, *arrays = lax.optimization_barrier((after, *arrays))
    tiles = [(arrays[i], index) for i, index in at]
    if aligned:
        _, pts, nc = arrays[0].shape
        outs = pl.pallas_call(
            functools.partial(gather_kernel, ntop, len(arrays), at[:nblk * ntop], at[nblk * ntop:]),
            out_shape=[jax.ShapeDtypeStruct((3 * nblk * pts, nc), jnp.bfloat16)] * ntop
            + [jax.ShapeDtypeStruct((nblk, nv, pts), jnp.float32)] * 2,
            in_specs=[SMEM] + [VMEM] * len(arrays),
            out_specs=[VMEM] * (ntop + 2),
            compiler_params=PARAMS,
            cost_estimate=COST,
        )(core.astype(jnp.int32)[None], *arrays)
        return after, outs[ntop:], outs[:ntop]
    tiles = [array[index] for array, index in tiles]
    rows = jnp.stack(tiles[nblk * ntop:]).reshape(nblk, 2, nv, -1)
    vals = [jnp.where(core == k, rows[:, 0], rows[:, 1]) for k in range(2)]
    return after, vals, [jnp.stack(tiles[a * nblk:(a + 1) * nblk]) for a in range(ntop)]


def apply_kernel(nchip, start, pair_ref, *refs):
    pots, (val_ref, right, out_ref, left) = refs[:nchip], refs[nchip:]
    nb, nv, nc = out_ref.shape
    pts = val_ref.shape[2]
    pair = pair_ref[0]
    vecs = pots[0].shape[0] // 2
    for j in range(nchip):
        both = pots[j][...]
        for e in range(2):
            g = e * nchip + j
            pot = jnp.where((pair ^ e) == 0, both[:vecs], both[vecs:])
            rows = val_ref[g]
            for b in range(nb):
                high, low = split(rows * pot[start + b:start + b + 1])
                at = pl.ds(b * nv, nv)
                left[at, pl.ds(3 * g * pts, pts)] = high
                left[at, pl.ds((3 * g + 1) * pts, pts)] = high
                left[at, pl.ds((3 * g + 2) * pts, pts)] = low
    total = jnp.dot(left[...], right[...], preferred_element_type=jnp.float32)
    out_ref[...] = total.reshape(nb, nv, nc)


def applied(aligned, pair, pots, val, con, start, shape):
    nb, nv, nc = shape
    nblk = val.shape[0]
    nchip = nblk // 2
    pts = pots[0].shape[1]
    if aligned:
        return pl.pallas_call(
            functools.partial(apply_kernel, nchip, start),
            out_shape=jax.ShapeDtypeStruct(shape, jnp.float32),
            in_specs=[SMEM] + [VMEM] * (nchip + 2),
            out_specs=VMEM,
            scratch_shapes=[pltpu.VMEM((nb * nv, 3 * nblk * pts), jnp.bfloat16)],
            compiler_params=PARAMS,
            cost_estimate=COST,
        )(pair.astype(jnp.int32)[None], *pots, val, con)
    pot = relative(jnp.stack(pots).reshape(nchip, 2, -1, pts), 1, pair)[:, :, start:start + nb]
    pot = jnp.transpose(pot, (1, 0, 2, 3)).reshape(nblk, nb, pts)
    return jnp.einsum("gvp,gbp,gpc->bvc", val.reshape(nblk, nv, pts), pot, con.reshape(nblk, pts, nc), precision=HIGH)


def make(nchip, ntop):
    def rc_swap(x, mask):
        return swap(x, "rc", nchip, mask)

    def top_swap(x, mask):
        return swap(x, "top", ntop, mask)

    def pair_swap(x):
        return swap(x, "pair", 2, 1)

    def core_swap(x):
        return swap(x, "core", 2, 1)

    def col_swap(x, mask):
        n = 2 * ntop
        return lax.ppermute(x, ("top", "pair"), [(i, i ^ mask) for i in range(n)])

    def relay(tiles, j):
        high = 1 << (j.bit_length() - 1)
        low = j & -j
        out = []
        for a in range(ntop):
            mask = low if a % 2 else high
            array, index = tiles[j ^ mask][a]
            out.append((rc_swap(array[index:index + 1], mask), 0))
        return out

    def per_device(x_pairs, eps_val, eps_con, orb_val, orb_con, screened_w):
        rc = lax.axis_index("rc")
        core = lax.axis_index("core")
        top = lax.axis_index("top")
        pair = lax.axis_index("pair")
        nb, nv, nc = x_pairs.shape
        pts = orb_val.shape[0]
        aligned = nc % 128 == 0 and pts == nc and 2 * nv == nc

        packed = pack(nchip, ntop, aligned, rc, top, pair, orb_con, orb_val, nc)
        from_pair = pair_swap(packed[0])
        from_chip = {j: rc_swap(packed[j], j) for j in range(1, nchip)}
        x_tops = [x_pairs] + [top_swap(x_pairs, a) for a in range(1, ntop)]
        from_pair, from_chip = lax.optimization_barrier((from_pair, from_chip))

        val = [{0: (packed[-1], 0)}, {}]
        con = [{0: [(packed[1], a) for a in range(ntop)]}, {0: [(from_pair, a) for a in range(ntop)]}]
        singles = [j for j in range(1, nchip) if single(j)]
        others = [j for j in range(1, nchip) if not single(j)]
        for j in range(1, nchip):
            val[0][j] = (from_chip[j], from_chip[j].shape[0] - 1)
            if single(j):
                con[0][j] = [(from_chip[j], a) for a in range(ntop)]

        def pair_val(part):
            got = pair_swap(jnp.stack([val[0][j][0][val[0][j][1]] for j in part]))
            for i, j in enumerate(part):
                val[1][j] = (got, i)

        pair_val([0] + singles)
        for j in singles:
            got = rc_swap(from_pair, j)
            con[1][j] = [(got, a) for a in range(ntop)]
        x = [[t, core_swap(t)] for t in x_tops]
        held = [con[0][j][0][0] for j in singles]
        x, held = lax.optimization_barrier((x, held))
        late = {j: [(held[i], index) for _, index in con[0][j]] for i, j in enumerate(singles)}
        for j in others:
            late[j] = relay(late, j)
            con[0][j] = late[j]
        if aligned:
            x = halves(x)
        else:
            x = [jnp.where(core == 0, jnp.stack(row, 1), jnp.stack(row[::-1], 1)) for row in x]

        def density(group):
            return densities(
                aligned, core, x_pairs.shape, x, [con[e][j] for e, j in group], [val[e][j] for e, j in group]
            )

        groups = [[(0, 0)] + [(0, j) for j in singles]]
        dens = [density(groups[0])]
        if others:
            arrays = [con[1][j][0][0] for j in singles] + [val[0][j][0] for j in others]
            dens[0], arrays = ordered(dens[0], arrays)
            con[1].update({j: [(arrays[i], index) for _, index in con[1][j]] for i, j in enumerate(singles)})
            for i, j in enumerate(others):
                val[0][j] = (arrays[len(singles) + i], val[0][j][1])
            for j in others:
                con[1][j] = relay(con[1], j)
            pair_val(others)
        groups.append([(1, 0)] + [(1, j) for j in singles])
        dens.append(density(groups[1]))
        if others:
            across = [con[0][j][a][0] for j in others for a in range(ntop)]
            dens[1], across = ordered(dens[1], across)
            for i, j in enumerate(others):
                con[0][j] = [(across[i * ntop + a], con[0][j][a][1]) for a in range(ntop)]
            groups += [[(0, j) for j in others], [(1, j) for j in others]]
            dens += [density(group) for group in groups[2:]]
        order = [e * nchip + j for group in groups for e, j in group]
        part = route(aligned, nchip, rc, pair, order, dens)
        got = lax.all_to_all(part, ("rc", "core", "top", "pair"), 0, 0, tiled=True)
        rows = screen(aligned, nchip, ntop, top, got, screened_w)
        vals = [val[e][j] for e in range(2) for j in range(nchip)]
        cons = [[con[e][j][a] for e in range(2) for j in range(nchip)] for a in range(ntop)]
        rows = list(rows)
        rows[0], vals, cons = gathered(aligned, core, rows[0], vals, cons, nv)
        row = rows[0]
        for d in range(1, 2 * ntop):
            row = row + col_swap(rows[d // 2], d)
        pots = [row] + [rc_swap(row, j) for j in range(1, nchip)]

        def apply(a, k, start, count):
            return applied(aligned, pair, pots, vals[k], cons[a], start, (count, nv, nc))

        def from_core(away):
            return jnp.concatenate([core_swap(away[i:i + 1]) for i in range(away.shape[0])], axis=0)

        base = (eps_con[None, None, :] - eps_val[None, :, None]) * x_pairs
        half = nb // 2
        sent = []
        for a in range(1, ntop):
            pieces = []
            for start in (0, half):
                away, step = apply(a, 1, start, half), apply(a, 0, start, half)
                step, pots[0] = lax.optimization_barrier((step + from_core(away), pots[0]))
                pieces.append(top_swap(step, a))
            sent = [s + p for s, p in zip(sent, pieces)] if sent else pieces
        away, step = apply(0, 1, 0, nb), apply(0, 0, 0, nb)
        base = lax.optimization_barrier(base + step + from_core(away))
        return base + jnp.concatenate(sent, axis=0) if sent else base

    return per_device


def solution(mesh):
    nrow, ncol = mesh.shape["rowpt"], mesh.shape["colpt"]
    nchip, ntop = nrow // 2, ncol // 2
    fine = Mesh(mesh.devices.reshape(nchip, 2, ntop, 2), ("rc", "core", "top", "pair"))
    row, col = ("rc", "core"), ("top", "pair")
    in_specs = (P(None, row, col), P(row), P(col), P(row + col, None), P(row + col, None), P(row, col))
    return jax.shard_map(
        make(nchip, ntop), mesh=fine, in_specs=in_specs, out_specs=P(None, row, col), check_vma=False
    )
```

```python
import functools

import jax
import jax.numpy as jnp
from jax import lax
from jax.experimental import pallas as pl
from jax.experimental.pallas import tpu as pltpu
from jax.sharding import Mesh, PartitionSpec as P

HIGH = lax.Precision.HIGH
VMEM = pl.BlockSpec(memory_space=pltpu.VMEM)
ANY = pl.BlockSpec(memory_space=pl.ANY)
SMEM = pl.BlockSpec(memory_space=pltpu.SMEM)
COST = pl.CostEstimate(flops=2 * 10**9, bytes_accessed=4 * 2**20, transcendentals=0)
PARAMS = pltpu.CompilerParams(vmem_limit_bytes=14 * 1024 * 1024)


def swap(x, axis, size, mask):
    return lax.ppermute(x, axis, [(i, i ^ mask) for i in range(size)])


def relative(x, axis, index):
    size = x.shape[axis]
    bit = 1
    while bit < size:
        shape = x.shape[:axis] + (size // (2 * bit), 2, bit) + x.shape[axis + 1:]
        flipped = jnp.flip(x.reshape(shape), axis + 1).reshape(x.shape)
        x = jnp.where((index & bit) != 0, flipped, x)
        bit *= 2
    return x


def ordered(first, then):
    return lax.optimization_barrier((first, then))


def single(j):
    return j & (j - 1) == 0


def split(x):
    high = x.astype(jnp.bfloat16)
    return high, (x - high.astype(jnp.float32)).astype(jnp.bfloat16)


def pack_kernel(nchip, ntop, where, con_ref, val_ref, *outs):
    nc = outs[0].shape[2]
    rc, top, pair = where[0], where[1], where[2]

    def con_tile(a, e):
        at = ((top ^ a) * 2 + (pair ^ e)) * nc
        return con_ref[:, pl.ds(pl.multiple_of(at, nc), nc)]

    def val_tile(j):
        at = (rc ^ j) * nc
        return val_ref[:, pl.ds(pl.multiple_of(at, nc), nc)].T

    for j in range(nchip + 1):
        out = outs[j]
        if j == 0 or (j < nchip and single(j)):
            for a in range(ntop):
                out[a] = con_tile(a, int(j == 0))
        if j:
            out[out.shape[0] - 1] = val_tile(j % nchip)


def pack(nchip, ntop, aligned, rc, top, pair, orb_con, orb_val, nc):
    pts = orb_con.shape[0]
    if aligned:
        sizes = [ntop] + [ntop + 1 if single(j) else 1 for j in range(1, nchip)] + [1]
        return pl.pallas_call(
            functools.partial(pack_kernel, nchip, ntop),
            out_shape=[jax.ShapeDtypeStruct((s, pts, nc), jnp.float32) for s in sizes],
            in_specs=[SMEM, VMEM, VMEM],
            out_specs=[VMEM] * (nchip + 1),
            compiler_params=PARAMS,
            cost_estimate=COST,
        )(jnp.stack([rc, top, pair]).astype(jnp.int32), orb_con, orb_val)

    def con_tile(a, e):
        return lax.dynamic_slice_in_dim(orb_con, ((top ^ a) * 2 + (pair ^ e)) * nc, nc, 1)

    def val_tile(j):
        return lax.dynamic_slice_in_dim(orb_val, (rc ^ j) * nc, nc, 1).T.reshape(pts, nc)

    out = [jnp.stack([con_tile(a, 1) for a in range(ntop)])]
    for j in range(1, nchip):
        con = [con_tile(a, 0) for a in range(ntop)] if single(j) else []
        out.append(jnp.stack(con + [val_tile(j)]))
    return out + [val_tile(0)[None]]


def operands(tiles):
    arrays, at = [], []
    for array, index in tiles:
        where = [i for i, other in enumerate(arrays) if other is array]
        if not where:
            arrays.append(array)
            where = [len(arrays) - 1]
        at.append((where[0], index))
    return arrays, at


def halves_kernel(x_refs, out_ref):
    nb, nv, nc = x_refs[0].shape
    width = out_ref.shape[1] // 2
    for i, ref in enumerate(x_refs):
        a, k = i // 2, i % 2
        high, low = split(ref[...].reshape(nb * nv, nc))
        rows = pl.ds(k * nb * nv, nb * nv)
        out_ref[rows, pl.ds(a * nc, nc)] = high
        out_ref[rows, pl.ds(width + a * nc, nc)] = low


def halves(x):
    flat = [t for row in x for t in row]
    nb, nv, nc = flat[0].shape
    return pl.pallas_call(
        lambda *refs: halves_kernel(refs[:-1], refs[-1]),
        out_shape=jax.ShapeDtypeStruct((2 * nb * nv, 2 * len(x) * nc), jnp.bfloat16),
        in_specs=[VMEM] * len(flat),
        out_specs=VMEM,
        compiler_params=PARAMS,
        cost_estimate=COST,
    )(*flat)


def density_kernel(nblk, ntop, shape, con_at, val_at, core_ref, x_ref, *refs):
    tiles, (dens_ref, right) = refs[:-2], refs[-2:]
    nb, nv, nc = shape
    width = ntop * nc
    core = core_ref[0]
    for g in range(nblk):
        for a in range(ntop):
            array, index = con_at[g * ntop + a]
            high, low = split(tiles[array][index])
            right[g, :, pl.ds(a * nc, nc)] = high
            right[g, :, pl.ds(width + a * nc, nc)] = high
            right[g, :, pl.ds(2 * width + a * nc, nc)] = low
        array, index = val_at[g]
        total = None
        for k in range(2):
            at = pl.ds(k * nb * nv, nb * nv)
            left = jnp.concatenate([x_ref[at, :], x_ref[at, pl.ds(0, width)]], axis=1)
            through = lax.dot_general(
                left, right[g], (((1,), (1,)), ((), ())), preferred_element_type=jnp.float32
            )
            rows = tiles[array][index, pl.ds(pl.multiple_of((core ^ k) * nv, nv), nv), :]
            part = jnp.sum(through.reshape(nb, nv, -1) * rows[None], axis=1)
            total = part if total is None else total + part
        dens_ref[g] = total


def densities(aligned, core, shape, x, con, val):
    nblk, ntop = len(con), len(con[0])
    nb, nv, nc = shape
    if aligned:
        arrays, at = operands([t for row in con for t in row] + list(val))
        pts = arrays[0].shape[1]
        return pl.pallas_call(
            functools.partial(density_kernel, nblk, ntop, shape, at[:nblk * ntop], at[nblk * ntop:]),
            out_shape=jax.ShapeDtypeStruct((nblk, nb, pts), jnp.float32),
            in_specs=[SMEM] + [VMEM] * (1 + len(arrays)),
            out_specs=VMEM,
            scratch_shapes=[pltpu.VMEM((nblk, pts, 3 * ntop * nc), jnp.bfloat16)],
            compiler_params=PARAMS,
            cost_estimate=COST,
        )(core.astype(jnp.int32)[None], x, *arrays)
    out = []
    for g in range(nblk):
        through = 0.0
        for a in range(ntop):
            array, index = con[g][a]
            through = through + jnp.einsum("bkvc,pc->bkvp", x[a], array[index], precision=HIGH)
        array, index = val[g]
        out.append(jnp.sum(through * array[index].reshape(1, 2, nv, -1), axis=(1, 2)))
    return jnp.stack(out)


def route_kernel(order, nchip, where, *refs):
    groups, out_ref, held = refs[:-2], refs[-2], refs[-1]
    nb = held.shape[1]
    rc, pair = where[0], where[1]
    at = 0
    for ref in groups:
        for g in range(ref.shape[0]):
            held[order[at]] = ref[g]
            at += 1
    for z in range(nchip):
        for p in range(2):
            piece = held[(pair ^ p) * nchip + (rc ^ z)]
            for d in range(out_ref.shape[0] // nchip):
                out_ref[d * nchip + z, pl.ds(p * nb, nb), :] = piece


def route(aligned, nchip, rc, pair, order, groups):
    nb, pts = groups[0].shape[1:]
    if aligned:
        return pl.pallas_call(
            functools.partial(route_kernel, order, nchip),
            out_shape=jax.ShapeDtypeStruct((2 * nchip * nchip, 2 * nb, pts), jnp.float32),
            in_specs=[SMEM] + [VMEM] * len(groups),
            out_specs=VMEM,
            scratch_shapes=[pltpu.VMEM((2 * nchip, nb, pts), jnp.float32)],
            compiler_params=PARAMS,
            cost_estimate=COST,
        )(jnp.stack([rc, pair]).astype(jnp.int32), *groups)
    flat = jnp.concatenate(groups)
    flat = jnp.stack([flat[order.index(i)] for i in range(2 * nchip)]).reshape(2, nchip, nb, pts)
    flat = jnp.transpose(relative(relative(flat, 1, rc), 0, pair), (1, 0, 2, 3)).reshape(nchip, 2 * nb, pts)
    return jnp.tile(flat, (2 * nchip, 1, 1))


def screen_kernel(nchip, ntop, top_ref, got_ref, w_ref, *refs):
    outs, (dens, left) = refs[:ntop], refs[ntop:]
    nb = got_ref.shape[1] // 2
    pts = got_ref.shape[2]
    top = top_ref[0]
    for k in range(2):
        for t in range(ntop):
            total = None
            for r in range(nchip):
                for p in range(2):
                    piece = got_ref[((r * 2 + k) * ntop + t) * 2 + p]
                    total = piece if total is None else total + piece
            for p in range(2):
                dens[:, pl.ds(((k * ntop + t) * 2 + p) * pts, pts)] = total[p * nb:(p + 1) * nb]
    high, low = split(dens[...])
    left[...] = jnp.zeros_like(left)
    left[pl.ds(0, nb), :] = high
    left[pl.ds(nb, nb), :] = low
    for a in range(ntop):
        for p in range(2):
            at = pl.multiple_of(((top ^ a) * 2 + p) * pts, pts)
            high, low = split(w_ref[pl.ds(at, pts), :])
            dims = (((1,), (1,)), ((), ()))
            total = lax.dot_general(left[...], high, dims, preferred_element_type=jnp.float32)
            extra = lax.dot_general(left[...], low, dims, preferred_element_type=jnp.float32)
            outs[a][pl.ds(p * nb, nb), :] = total[:nb] + total[nb:2 * nb] + extra[:nb]


def screen(aligned, nchip, ntop, top, got, screened_w):
    nb, pts = got.shape[1] // 2, got.shape[2]
    if aligned:
        nq = screened_w.shape[1]
        return pl.pallas_call(
            functools.partial(screen_kernel, nchip, ntop),
            out_shape=[jax.ShapeDtypeStruct((2 * nb, pts), jnp.float32)] * ntop,
            in_specs=[SMEM, VMEM, VMEM],
            out_specs=[VMEM] * ntop,
            scratch_shapes=[pltpu.VMEM((nb, nq), jnp.float32), pltpu.VMEM((16, nq), jnp.bfloat16)],
            compiler_params=PARAMS,
            cost_estimate=COST,
        )(top.astype(jnp.int32)[None], got, screened_w)
    density = jnp.sum(got.reshape(nchip, 2, ntop, 2, 2, nb, pts), axis=(0, 3))
    density = jnp.transpose(density.reshape(-1, nb, pts), (1, 0, 2)).reshape(nb, -1)
    rows = lax.dot_general(density, screened_w, (((1,), (1,)), ((), ())), precision=HIGH)
    rows = jnp.transpose(rows.reshape(nb, ntop, 2, pts), (1, 2, 0, 3)).reshape(ntop, 2 * nb, pts)
    rows = relative(rows, 0, top)
    return [rows[a] for a in range(ntop)]


def gather_kernel(ntop, nin, con_at, val_at, core_ref, *refs):
    tiles, rights, val_refs = refs[:nin], refs[nin:nin + ntop], refs[nin + ntop:]
    nblk, nv, pts = val_refs[0].shape
    core = core_ref[0]
    for g in range(nblk):
        for a in range(ntop):
            array, index = con_at[a * nblk + g]
            high, low = split(tiles[array][index])
            rights[a][pl.ds(3 * g * pts, pts), :] = high
            rights[a][pl.ds((3 * g + 1) * pts, pts), :] = low
            rights[a][pl.ds((3 * g + 2) * pts, pts), :] = high
        array, index = val_at[g]
        for k in range(2):
            val_refs[k][g] = tiles[array][index, pl.ds(pl.multiple_of((core ^ k) * nv, nv), nv), :]


def gathered(aligned, core, after, val, con, nv):
    nblk, ntop = len(val), len(con)
    arrays, at = operands([t for row in con for t in row] + val)
    after, *arrays = lax.optimization_barrier((after, *arrays))
    tiles = [(arrays[i], index) for i, index in at]
    if aligned:
        _, pts, nc = arrays[0].shape
        outs = pl.pallas_call(
            functools.partial(gather_kernel, ntop, len(arrays), at[:nblk * ntop], at[nblk * ntop:]),
            out_shape=[jax.ShapeDtypeStruct((3 * nblk * pts, nc), jnp.bfloat16)] * ntop
            + [jax.ShapeDtypeStruct((nblk, nv, pts), jnp.float32)] * 2,
            in_specs=[SMEM] + [VMEM] * len(arrays),
            out_specs=[VMEM] * (ntop + 2),
            compiler_params=PARAMS,
            cost_estimate=COST,
        )(core.astype(jnp.int32)[None], *arrays)
        return after, outs[ntop:], outs[:ntop]
    tiles = [array[index] for array, index in tiles]
    rows = jnp.stack(tiles[nblk * ntop:]).reshape(nblk, 2, nv, -1)
    vals = [jnp.where(core == k, rows[:, 0], rows[:, 1]) for k in range(2)]
    return after, vals, [jnp.stack(tiles[a * nblk:(a + 1) * nblk]) for a in range(ntop)]


def apply_kernel(nchip, start, pair_ref, *refs):
    pots, (val_ref, right), (out_ref, left) = refs[:nchip], refs[nchip:nchip + 2], refs[-2:]
    nb, nv, nc = out_ref.shape
    pts = val_ref.shape[2]
    pair = pair_ref[0]
    vecs = pots[0].shape[0] // 2
    for j in range(nchip):
        both = pots[j][...]
        for e in range(2):
            g = e * nchip + j
            pot = jnp.where((pair ^ e) == 0, both[:vecs], both[vecs:])
            rows = val_ref[g]
            for b in range(nb):
                high, low = split(rows * pot[start + b:start + b + 1])
                at = pl.ds(b * nv, nv)
                left[at, pl.ds(3 * g * pts, pts)] = high
                left[at, pl.ds((3 * g + 1) * pts, pts)] = high
                left[at, pl.ds((3 * g + 2) * pts, pts)] = low
    total = jnp.dot(left[...], right[...], preferred_element_type=jnp.float32)
    out_ref[...] = total.reshape(nb, nv, nc)


def applied(aligned, pair, pots, val, con, start, shape, after=()):
    nb, nv, nc = shape
    nblk = val.shape[0]
    nchip = nblk // 2
    pts = pots[0].shape[1]
    if aligned:
        return pl.pallas_call(
            functools.partial(apply_kernel, nchip, start),
            out_shape=jax.ShapeDtypeStruct(shape, jnp.float32),
            in_specs=[SMEM] + [VMEM] * (nchip + 2) + [ANY] * len(after),
            out_specs=VMEM,
            scratch_shapes=[pltpu.VMEM((nb * nv, 3 * nblk * pts), jnp.bfloat16)],
            compiler_params=PARAMS,
            cost_estimate=COST,
        )(pair.astype(jnp.int32)[None], *pots, val, con, *after)
    pot = relative(jnp.stack(pots).reshape(nchip, 2, -1, pts), 1, pair)[:, :, start:start + nb]
    pot = jnp.transpose(pot, (1, 0, 2, 3)).reshape(nblk, nb, pts)
    return jnp.einsum("gvp,gbp,gpc->bvc", val.reshape(nblk, nv, pts), pot, con.reshape(nblk, pts, nc), precision=HIGH)


def make(nchip, ntop):
    def rc_swap(x, mask):
        return swap(x, "rc", nchip, mask)

    def top_swap(x, mask):
        return swap(x, "top", ntop, mask)

    def pair_swap(x):
        return swap(x, "pair", 2, 1)

    def core_swap(x):
        return swap(x, "core", 2, 1)

    def col_swap(x, mask):
        n = 2 * ntop
        return lax.ppermute(x, ("top", "pair"), [(i, i ^ mask) for i in range(n)])

    def relay(tiles, j):
        high = 1 << (j.bit_length() - 1)
        low = j & -j
        out = []
        for a in range(ntop):
            mask = low if a % 2 else high
            array, index = tiles[j ^ mask][a]
            out.append((rc_swap(array[index:index + 1], mask), 0))
        return out

    def per_device(x_pairs, eps_val, eps_con, orb_val, orb_con, screened_w):
        rc = lax.axis_index("rc")
        core = lax.axis_index("core")
        top = lax.axis_index("top")
        pair = lax.axis_index("pair")
        nb, nv, nc = x_pairs.shape
        pts = orb_val.shape[0]
        aligned = nc % 128 == 0 and pts == nc and 2 * nv == nc

        packed = pack(nchip, ntop, aligned, rc, top, pair, orb_con, orb_val, nc)
        from_pair = pair_swap(packed[0])
        from_chip = {j: rc_swap(packed[j], j) for j in range(1, nchip)}
        x_tops = [x_pairs] + [top_swap(x_pairs, a) for a in range(1, ntop)]
        from_pair, from_chip = lax.optimization_barrier((from_pair, from_chip))

        val = [{0: (packed[-1], 0)}, {}]
        con = [{0: [(packed[1], a) for a in range(ntop)]}, {0: [(from_pair, a) for a in range(ntop)]}]
        singles = [j for j in range(1, nchip) if single(j)]
        others = [j for j in range(1, nchip) if not single(j)]
        for j in range(1, nchip):
            val[0][j] = (from_chip[j], from_chip[j].shape[0] - 1)
            if single(j):
                con[0][j] = [(from_chip[j], a) for a in range(ntop)]

        def pair_val(part):
            got = pair_swap(jnp.stack([val[0][j][0][val[0][j][1]] for j in part]))
            for i, j in enumerate(part):
                val[1][j] = (got, i)

        pair_val([0] + singles)
        for j in singles:
            got = rc_swap(from_pair, j)
            con[1][j] = [(got, a) for a in range(ntop)]
        x = [[t, core_swap(t)] for t in x_tops]
        held = [con[0][j][0][0] for j in singles]
        x, held = lax.optimization_barrier((x, held))
        late = {j: [(held[i], index) for _, index in con[0][j]] for i, j in enumerate(singles)}
        for j in others:
            late[j] = relay(late, j)
            con[0][j] = late[j]
        if aligned:
            x = halves(x)
        else:
            x = [jnp.where(core == 0, jnp.stack(row, 1), jnp.stack(row[::-1], 1)) for row in x]

        def density(group):
            return densities(
                aligned, core, x_pairs.shape, x, [con[e][j] for e, j in group], [val[e][j] for e, j in group]
            )

        groups = [[(0, 0)] + [(0, j) for j in singles]]
        dens = [density(groups[0])]
        if others:
            arrays = [con[1][j][0][0] for j in singles] + [val[0][j][0] for j in others]
            dens[0], arrays = ordered(dens[0], arrays)
            con[1].update({j: [(arrays[i], index) for _, index in con[1][j]] for i, j in enumerate(singles)})
            for i, j in enumerate(others):
                val[0][j] = (arrays[len(singles) + i], val[0][j][1])
            for j in others:
                con[1][j] = relay(con[1], j)
            pair_val(others)
        groups.append([(1, 0)] + [(1, j) for j in singles])
        dens.append(density(groups[1]))
        if others:
            across = [con[0][j][a][0] for j in others for a in range(ntop)]
            dens[1], across = ordered(dens[1], across)
            for i, j in enumerate(others):
                con[0][j] = [(across[i * ntop + a], con[0][j][a][1]) for a in range(ntop)]
            groups += [[(0, j) for j in others], [(1, j) for j in others]]
            dens += [density(group) for group in groups[2:]]
        order = [e * nchip + j for group in groups for e, j in group]
        part = route(aligned, nchip, rc, pair, order, dens)
        got = lax.all_to_all(part, ("rc", "core", "top", "pair"), 0, 0, tiled=True)
        rows = screen(aligned, nchip, ntop, top, got, screened_w)
        vals = [val[e][j] for e in range(2) for j in range(nchip)]
        cons = [[con[e][j][a] for e in range(2) for j in range(nchip)] for a in range(ntop)]
        rows = list(rows)
        rows[0], vals, cons = gathered(aligned, core, rows[0], vals, cons, nv)
        row = rows[0]
        for d in range(1, 2 * ntop):
            row = row + col_swap(rows[d // 2], d)
        pots = [row] + [rc_swap(row, j) for j in range(1, nchip)]

        def apply(a, k, start, count, after=()):
            return applied(aligned, pair, pots, vals[k], cons[a], start, (count, nv, nc), after)

        def from_core(away):
            return jnp.concatenate([core_swap(away[i:i + 1]) for i in range(away.shape[0])], axis=0)

        base = (eps_con[None, None, :] - eps_val[None, :, None]) * x_pairs
        half = nb // 2
        sent = []
        for a in range(1, ntop):
            pieces = []
            after = ()
            for start in (0, half):
                away, step = apply(a, 1, start, half, after), apply(a, 0, start, half, after)
                step, pots[0] = lax.optimization_barrier((step + from_core(away), pots[0]))
                pieces.append(top_swap(step, a))
                after = (core_swap(step[0, :8, :128]),)
            sent = [s + p for s, p in zip(sent, pieces)] if sent else pieces
        away, step = apply(0, 1, 0, nb), apply(0, 0, 0, nb)
        base = lax.optimization_barrier(base + step + from_core(away))
        return base + jnp.concatenate(sent, axis=0) if sent else base

    return per_device


def solution(mesh):
    nrow, ncol = mesh.shape["rowpt"], mesh.shape["colpt"]
    nchip, ntop = nrow // 2, ncol // 2
    fine = Mesh(mesh.devices.reshape(nchip, 2, ntop, 2), ("rc", "core", "top", "pair"))
    row, col = ("rc", "core"), ("top", "pair")
    in_specs = (P(None, row, col), P(row), P(col), P(row + col, None), P(row + col, None), P(row, col))
    return jax.shard_map(
        make(nchip, ntop), mesh=fine, in_specs=in_specs, out_specs=P(None, row, col), check_vma=False
    )
```

```python
import functools

import jax
import jax.numpy as jnp
from jax import lax
from jax.experimental import pallas as pl
from jax.experimental.pallas import tpu as pltpu
from jax.sharding import Mesh, PartitionSpec as P

HIGH = lax.Precision.HIGH
VMEM = pl.BlockSpec(memory_space=pltpu.VMEM)
ANY = pl.BlockSpec(memory_space=pl.ANY)
SMEM = pl.BlockSpec(memory_space=pltpu.SMEM)
COST = pl.CostEstimate(flops=2 * 10**9, bytes_accessed=4 * 2**20, transcendentals=0)
PARAMS = pltpu.CompilerParams(vmem_limit_bytes=14 * 1024 * 1024)


def swap(x, axis, size, mask):
    return lax.ppermute(x, axis, [(i, i ^ mask) for i in range(size)])


def relative(x, axis, index):
    size = x.shape[axis]
    bit = 1
    while bit < size:
        shape = x.shape[:axis] + (size // (2 * bit), 2, bit) + x.shape[axis + 1:]
        flipped = jnp.flip(x.reshape(shape), axis + 1).reshape(x.shape)
        x = jnp.where((index & bit) != 0, flipped, x)
        bit *= 2
    return x


def ordered(first, then):
    return lax.optimization_barrier((first, then))


def single(j):
    return j & (j - 1) == 0


def split(x):
    high = x.astype(jnp.bfloat16)
    return high, (x - high.astype(jnp.float32)).astype(jnp.bfloat16)


def pack_kernel(nchip, ntop, where, con_ref, val_ref, *outs):
    nc = outs[0].shape[2]
    rc, top, pair = where[0], where[1], where[2]

    def con_tile(a, e):
        at = ((top ^ a) * 2 + (pair ^ e)) * nc
        return con_ref[:, pl.ds(pl.multiple_of(at, nc), nc)]

    def val_tile(j):
        at = (rc ^ j) * nc
        return val_ref[:, pl.ds(pl.multiple_of(at, nc), nc)].T

    for j in range(nchip + 1):
        out = outs[j]
        if j == 0 or (j < nchip and single(j)):
            for a in range(ntop):
                out[a] = con_tile(a, int(j == 0))
        if j:
            out[out.shape[0] - 1] = val_tile(j % nchip)


def pack(nchip, ntop, aligned, rc, top, pair, orb_con, orb_val, nc):
    pts = orb_con.shape[0]
    if aligned:
        sizes = [ntop] + [ntop + 1 if single(j) else 1 for j in range(1, nchip)] + [1]
        return pl.pallas_call(
            functools.partial(pack_kernel, nchip, ntop),
            out_shape=[jax.ShapeDtypeStruct((s, pts, nc), jnp.float32) for s in sizes],
            in_specs=[SMEM, VMEM, VMEM],
            out_specs=[VMEM] * (nchip + 1),
            compiler_params=PARAMS,
            cost_estimate=COST,
        )(jnp.stack([rc, top, pair]).astype(jnp.int32), orb_con, orb_val)

    def con_tile(a, e):
        return lax.dynamic_slice_in_dim(orb_con, ((top ^ a) * 2 + (pair ^ e)) * nc, nc, 1)

    def val_tile(j):
        return lax.dynamic_slice_in_dim(orb_val, (rc ^ j) * nc, nc, 1).T.reshape(pts, nc)

    out = [jnp.stack([con_tile(a, 1) for a in range(ntop)])]
    for j in range(1, nchip):
        con = [con_tile(a, 0) for a in range(ntop)] if single(j) else []
        out.append(jnp.stack(con + [val_tile(j)]))
    return out + [val_tile(0)[None]]


def operands(tiles):
    arrays, at = [], []
    for array, index in tiles:
        where = [i for i, other in enumerate(arrays) if other is array]
        if not where:
            arrays.append(array)
            where = [len(arrays) - 1]
        at.append((where[0], index))
    return arrays, at


def halves_kernel(x_refs, out_ref):
    nb, nv, nc = x_refs[0].shape
    width = out_ref.shape[1] // 2
    for i, ref in enumerate(x_refs):
        a, k = i // 2, i % 2
        high, low = split(ref[...].reshape(nb * nv, nc))
        rows = pl.ds(k * nb * nv, nb * nv)
        out_ref[rows, pl.ds(a * nc, nc)] = high
        out_ref[rows, pl.ds(width + a * nc, nc)] = low


def halves(x):
    flat = [t for row in x for t in row]
    nb, nv, nc = flat[0].shape
    return pl.pallas_call(
        lambda *refs: halves_kernel(refs[:-1], refs[-1]),
        out_shape=jax.ShapeDtypeStruct((2 * nb * nv, 2 * len(x) * nc), jnp.bfloat16),
        in_specs=[VMEM] * len(flat),
        out_specs=VMEM,
        compiler_params=PARAMS,
        cost_estimate=COST,
    )(*flat)


def density_kernel(nblk, ntop, shape, con_at, val_at, core_ref, x_ref, *refs):
    tiles, (dens_ref, right) = refs[:-2], refs[-2:]
    nb, nv, nc = shape
    width = ntop * nc
    core = core_ref[0]
    for g in range(nblk):
        for a in range(ntop):
            array, index = con_at[g * ntop + a]
            high, low = split(tiles[array][index])
            right[g, :, pl.ds(a * nc, nc)] = high
            right[g, :, pl.ds(width + a * nc, nc)] = high
            right[g, :, pl.ds(2 * width + a * nc, nc)] = low
        array, index = val_at[g]
        total = None
        for k in range(2):
            at = pl.ds(k * nb * nv, nb * nv)
            left = jnp.concatenate([x_ref[at, :], x_ref[at, pl.ds(0, width)]], axis=1)
            through = lax.dot_general(
                left, right[g], (((1,), (1,)), ((), ())), preferred_element_type=jnp.float32
            )
            rows = tiles[array][index, pl.ds(pl.multiple_of((core ^ k) * nv, nv), nv), :]
            part = jnp.sum(through.reshape(nb, nv, -1) * rows[None], axis=1)
            total = part if total is None else total + part
        dens_ref[g] = total


def densities(aligned, core, shape, x, con, val):
    nblk, ntop = len(con), len(con[0])
    nb, nv, nc = shape
    if aligned:
        arrays, at = operands([t for row in con for t in row] + list(val))
        pts = arrays[0].shape[1]
        return pl.pallas_call(
            functools.partial(density_kernel, nblk, ntop, shape, at[:nblk * ntop], at[nblk * ntop:]),
            out_shape=jax.ShapeDtypeStruct((nblk, nb, pts), jnp.float32),
            in_specs=[SMEM] + [VMEM] * (1 + len(arrays)),
            out_specs=VMEM,
            scratch_shapes=[pltpu.VMEM((nblk, pts, 3 * ntop * nc), jnp.bfloat16)],
            compiler_params=PARAMS,
            cost_estimate=COST,
        )(core.astype(jnp.int32)[None], x, *arrays)
    out = []
    for g in range(nblk):
        through = 0.0
        for a in range(ntop):
            array, index = con[g][a]
            through = through + jnp.einsum("bkvc,pc->bkvp", x[a], array[index], precision=HIGH)
        array, index = val[g]
        out.append(jnp.sum(through * array[index].reshape(1, 2, nv, -1), axis=(1, 2)))
    return jnp.stack(out)


def route_kernel(order, nchip, where, *refs):
    groups, out_ref, held = refs[:-2], refs[-2], refs[-1]
    nb = held.shape[1]
    rc, pair = where[0], where[1]
    at = 0
    for ref in groups:
        for g in range(ref.shape[0]):
            held[order[at]] = ref[g]
            at += 1
    for z in range(nchip):
        for p in range(2):
            piece = held[(pair ^ p) * nchip + (rc ^ z)]
            for d in range(out_ref.shape[0] // nchip):
                out_ref[d * nchip + z, pl.ds(p * nb, nb), :] = piece


def route(aligned, nchip, rc, pair, order, groups):
    nb, pts = groups[0].shape[1:]
    if aligned:
        return pl.pallas_call(
            functools.partial(route_kernel, order, nchip),
            out_shape=jax.ShapeDtypeStruct((2 * nchip * nchip, 2 * nb, pts), jnp.float32),
            in_specs=[SMEM] + [VMEM] * len(groups),
            out_specs=VMEM,
            scratch_shapes=[pltpu.VMEM((2 * nchip, nb, pts), jnp.float32)],
            compiler_params=PARAMS,
            cost_estimate=COST,
        )(jnp.stack([rc, pair]).astype(jnp.int32), *groups)
    flat = jnp.concatenate(groups)
    flat = jnp.stack([flat[order.index(i)] for i in range(2 * nchip)]).reshape(2, nchip, nb, pts)
    flat = jnp.transpose(relative(relative(flat, 1, rc), 0, pair), (1, 0, 2, 3)).reshape(nchip, 2 * nb, pts)
    return jnp.tile(flat, (2 * nchip, 1, 1))


def screen_kernel(nchip, ntop, top_ref, got_ref, w_ref, *refs):
    outs, (dens, left) = refs[:ntop], refs[ntop:]
    nb = got_ref.shape[1] // 2
    pts = got_ref.shape[2]
    top = top_ref[0]
    for k in range(2):
        for t in range(ntop):
            total = None
            for r in range(nchip):
                for p in range(2):
                    piece = got_ref[((r * 2 + k) * ntop + t) * 2 + p]
                    total = piece if total is None else total + piece
            for p in range(2):
                dens[:, pl.ds(((k * ntop + t) * 2 + p) * pts, pts)] = total[p * nb:(p + 1) * nb]
    high, low = split(dens[...])
    left[...] = jnp.zeros_like(left)
    left[pl.ds(0, nb), :] = high
    left[pl.ds(nb, nb), :] = low
    for a in range(ntop):
        for p in range(2):
            at = pl.multiple_of(((top ^ a) * 2 + p) * pts, pts)
            high, low = split(w_ref[pl.ds(at, pts), :])
            dims = (((1,), (1,)), ((), ()))
            total = lax.dot_general(left[...], high, dims, preferred_element_type=jnp.float32)
            extra = lax.dot_general(left[...], low, dims, preferred_element_type=jnp.float32)
            outs[a][pl.ds(p * nb, nb), :] = total[:nb] + total[nb:2 * nb] + extra[:nb]


def screen(aligned, nchip, ntop, top, got, screened_w):
    nb, pts = got.shape[1] // 2, got.shape[2]
    if aligned:
        nq = screened_w.shape[1]
        return pl.pallas_call(
            functools.partial(screen_kernel, nchip, ntop),
            out_shape=[jax.ShapeDtypeStruct((2 * nb, pts), jnp.float32)] * ntop,
            in_specs=[SMEM, VMEM, VMEM],
            out_specs=[VMEM] * ntop,
            scratch_shapes=[pltpu.VMEM((nb, nq), jnp.float32), pltpu.VMEM((16, nq), jnp.bfloat16)],
            compiler_params=PARAMS,
            cost_estimate=COST,
        )(top.astype(jnp.int32)[None], got, screened_w)
    density = jnp.sum(got.reshape(nchip, 2, ntop, 2, 2, nb, pts), axis=(0, 3))
    density = jnp.transpose(density.reshape(-1, nb, pts), (1, 0, 2)).reshape(nb, -1)
    rows = lax.dot_general(density, screened_w, (((1,), (1,)), ((), ())), precision=HIGH)
    rows = jnp.transpose(rows.reshape(nb, ntop, 2, pts), (1, 2, 0, 3)).reshape(ntop, 2 * nb, pts)
    rows = relative(rows, 0, top)
    return [rows[a] for a in range(ntop)]


def gather_kernel(ntop, nin, con_at, val_at, core_ref, *refs):
    tiles, rights, val_refs = refs[:nin], refs[nin:nin + ntop], refs[nin + ntop:]
    nblk, nv, pts = val_refs[0].shape
    core = core_ref[0]
    for g in range(nblk):
        for a in range(ntop):
            array, index = con_at[a * nblk + g]
            high, low = split(tiles[array][index])
            rights[a][pl.ds(3 * g * pts, pts), :] = high
            rights[a][pl.ds((3 * g + 1) * pts, pts), :] = low
            rights[a][pl.ds((3 * g + 2) * pts, pts), :] = high
        array, index = val_at[g]
        for k in range(2):
            val_refs[k][g] = tiles[array][index, pl.ds(pl.multiple_of((core ^ k) * nv, nv), nv), :]


def gathered(aligned, core, after, val, con, nv):
    nblk, ntop = len(val), len(con)
    arrays, at = operands([t for row in con for t in row] + val)
    after, *arrays = lax.optimization_barrier((after, *arrays))
    tiles = [(arrays[i], index) for i, index in at]
    if aligned:
        _, pts, nc = arrays[0].shape
        outs = pl.pallas_call(
            functools.partial(gather_kernel, ntop, len(arrays), at[:nblk * ntop], at[nblk * ntop:]),
            out_shape=[jax.ShapeDtypeStruct((3 * nblk * pts, nc), jnp.bfloat16)] * ntop
            + [jax.ShapeDtypeStruct((nblk, nv, pts), jnp.float32)] * 2,
            in_specs=[SMEM] + [VMEM] * len(arrays),
            out_specs=[VMEM] * (ntop + 2),
            compiler_params=PARAMS,
            cost_estimate=COST,
        )(core.astype(jnp.int32)[None], *arrays)
        return after, outs[ntop:], outs[:ntop]
    tiles = [array[index] for array, index in tiles]
    rows = jnp.stack(tiles[nblk * ntop:]).reshape(nblk, 2, nv, -1)
    vals = [jnp.where(core == k, rows[:, 0], rows[:, 1]) for k in range(2)]
    return after, vals, [jnp.stack(tiles[a * nblk:(a + 1) * nblk]) for a in range(ntop)]


def apply_kernel(nchip, start, pair_ref, *refs):
    pots, (val_ref, right), (out_ref, left) = refs[:nchip], refs[nchip:nchip + 2], refs[-2:]
    nb, nv, nc = out_ref.shape
    pts = val_ref.shape[2]
    pair = pair_ref[0]
    vecs = pots[0].shape[0] // 2
    for j in range(nchip):
        both = pots[j][...]
        for e in range(2):
            g = e * nchip + j
            pot = jnp.where((pair ^ e) == 0, both[:vecs], both[vecs:])
            rows = val_ref[g]
            for b in range(nb):
                high, low = split(rows * pot[start + b:start + b + 1])
                at = pl.ds(b * nv, nv)
                left[at, pl.ds(3 * g * pts, pts)] = high
                left[at, pl.ds((3 * g + 1) * pts, pts)] = high
                left[at, pl.ds((3 * g + 2) * pts, pts)] = low
    total = jnp.dot(left[...], right[...], preferred_element_type=jnp.float32)
    out_ref[...] = total.reshape(nb, nv, nc)


def applied(aligned, pair, pots, val, con, start, shape, after=()):
    nb, nv, nc = shape
    nblk = val.shape[0]
    nchip = nblk // 2
    pts = pots[0].shape[1]
    if aligned:
        return pl.pallas_call(
            functools.partial(apply_kernel, nchip, start),
            out_shape=jax.ShapeDtypeStruct(shape, jnp.float32),
            in_specs=[SMEM] + [VMEM] * (nchip + 2) + [ANY] * len(after),
            out_specs=VMEM,
            scratch_shapes=[pltpu.VMEM((nb * nv, 3 * nblk * pts), jnp.bfloat16)],
            compiler_params=PARAMS,
            cost_estimate=COST,
        )(pair.astype(jnp.int32)[None], *pots, val, con, *after)
    pot = relative(jnp.stack(pots).reshape(nchip, 2, -1, pts), 1, pair)[:, :, start:start + nb]
    pot = jnp.transpose(pot, (1, 0, 2, 3)).reshape(nblk, nb, pts)
    return jnp.einsum("gvp,gbp,gpc->bvc", val.reshape(nblk, nv, pts), pot, con.reshape(nblk, pts, nc), precision=HIGH)


def make(nchip, ntop):
    def rc_swap(x, mask):
        return swap(x, "rc", nchip, mask)

    def top_swap(x, mask):
        return swap(x, "top", ntop, mask)

    def pair_swap(x):
        return swap(x, "pair", 2, 1)

    def core_swap(x):
        return swap(x, "core", 2, 1)

    def col_swap(x, mask):
        n = 2 * ntop
        return lax.ppermute(x, ("top", "pair"), [(i, i ^ mask) for i in range(n)])

    def relay(tiles, j):
        high = 1 << (j.bit_length() - 1)
        low = j & -j
        out = []
        for a in range(ntop):
            mask = low if a % 2 else high
            array, index = tiles[j ^ mask][a]
            out.append((rc_swap(array[index:index + 1], mask), 0))
        return out

    def per_device(x_pairs, eps_val, eps_con, orb_val, orb_con, screened_w):
        rc = lax.axis_index("rc")
        core = lax.axis_index("core")
        top = lax.axis_index("top")
        pair = lax.axis_index("pair")
        nb, nv, nc = x_pairs.shape
        pts = orb_val.shape[0]
        aligned = nc % 128 == 0 and pts == nc and 2 * nv == nc

        packed = pack(nchip, ntop, aligned, rc, top, pair, orb_con, orb_val, nc)
        from_pair = pair_swap(packed[0])
        from_chip = {j: rc_swap(packed[j], j) for j in range(1, nchip)}
        x_tops = [x_pairs] + [top_swap(x_pairs, a) for a in range(1, ntop)]
        from_pair, from_chip = lax.optimization_barrier((from_pair, from_chip))

        val = [{0: (packed[-1], 0)}, {}]
        con = [{0: [(packed[1], a) for a in range(ntop)]}, {0: [(from_pair, a) for a in range(ntop)]}]
        singles = [j for j in range(1, nchip) if single(j)]
        others = [j for j in range(1, nchip) if not single(j)]
        for j in range(1, nchip):
            val[0][j] = (from_chip[j], from_chip[j].shape[0] - 1)
            if single(j):
                con[0][j] = [(from_chip[j], a) for a in range(ntop)]

        def pair_val(part):
            got = pair_swap(jnp.stack([val[0][j][0][val[0][j][1]] for j in part]))
            for i, j in enumerate(part):
                val[1][j] = (got, i)

        pair_val([0] + singles)
        for j in singles:
            got = rc_swap(from_pair, j)
            con[1][j] = [(got, a) for a in range(ntop)]
        x = [[t, core_swap(t)] for t in x_tops]
        held = [con[0][j][0][0] for j in singles]
        x, held = lax.optimization_barrier((x, held))
        late = {j: [(held[i], index) for _, index in con[0][j]] for i, j in enumerate(singles)}
        for j in others:
            late[j] = relay(late, j)
            con[0][j] = late[j]
        if aligned:
            x = halves(x)
        else:
            x = [jnp.where(core == 0, jnp.stack(row, 1), jnp.stack(row[::-1], 1)) for row in x]

        def density(group):
            return densities(
                aligned, core, x_pairs.shape, x, [con[e][j] for e, j in group], [val[e][j] for e, j in group]
            )

        groups = [[(0, 0)] + [(0, j) for j in singles]]
        dens = [density(groups[0])]
        if others:
            arrays = [con[1][j][0][0] for j in singles]
            last = [val[0][j][0] for j in others]
            dens[0], last = ordered(dens[0], last)
            dens[0], arrays = ordered(dens[0], arrays)
            arrays = arrays + last
            con[1].update({j: [(arrays[i], index) for _, index in con[1][j]] for i, j in enumerate(singles)})
            for i, j in enumerate(others):
                val[0][j] = (arrays[len(singles) + i], val[0][j][1])
            for j in others:
                con[1][j] = relay(con[1], j)
            pair_val(others)
        groups.append([(1, 0)] + [(1, j) for j in singles])
        dens.append(density(groups[1]))
        if others:
            across = [con[0][j][a][0] for j in others for a in range(ntop)]
            dens[1], across = ordered(dens[1], across)
            for i, j in enumerate(others):
                con[0][j] = [(across[i * ntop + a], con[0][j][a][1]) for a in range(ntop)]
            groups += [[(0, j) for j in others], [(1, j) for j in others]]
            dens += [density(group) for group in groups[2:]]
        order = [e * nchip + j for group in groups for e, j in group]
        part = route(aligned, nchip, rc, pair, order, dens)
        got = lax.all_to_all(part, ("rc", "core", "top", "pair"), 0, 0, tiled=True)
        rows = screen(aligned, nchip, ntop, top, got, screened_w)
        vals = [val[e][j] for e in range(2) for j in range(nchip)]
        cons = [[con[e][j][a] for e in range(2) for j in range(nchip)] for a in range(ntop)]
        rows = list(rows)
        rows[0], vals, cons = gathered(aligned, core, rows[0], vals, cons, nv)
        row = rows[0]
        for d in range(1, 2 * ntop):
            row = row + col_swap(rows[d // 2], d)
        pots = [row] + [rc_swap(row, j) for j in range(1, nchip)]

        def apply(a, k, start, count, after=()):
            return applied(aligned, pair, pots, vals[k], cons[a], start, (count, nv, nc), after)

        def from_core(away):
            return jnp.concatenate([core_swap(away[i:i + 1]) for i in range(away.shape[0])], axis=0)

        base = (eps_con[None, None, :] - eps_val[None, :, None]) * x_pairs
        half = nb // 2
        sent = []
        for a in range(1, ntop):
            pieces = []
            after = ()
            for start in (0, half):
                away, step = apply(a, 1, start, half, after), apply(a, 0, start, half, after)
                step, pots[0] = lax.optimization_barrier((step + from_core(away), pots[0]))
                pieces.append(top_swap(step, a))
                after = (core_swap(step[0, :8, :128]),)
            sent = [s + p for s, p in zip(sent, pieces)] if sent else pieces
        away, step = apply(0, 1, 0, nb), apply(0, 0, 0, nb)
        base = lax.optimization_barrier(base + step + from_core(away))
        return base + jnp.concatenate(sent, axis=0) if sent else base

    return per_device


def solution(mesh):
    nrow, ncol = mesh.shape["rowpt"], mesh.shape["colpt"]
    nchip, ntop = nrow // 2, ncol // 2
    fine = Mesh(mesh.devices.reshape(nchip, 2, ntop, 2), ("rc", "core", "top", "pair"))
    row, col = ("rc", "core"), ("top", "pair")
    in_specs = (P(None, row, col), P(row), P(col), P(row + col, None), P(row + col, None), P(row, col))
    return jax.shard_map(
        make(nchip, ntop), mesh=fine, in_specs=in_specs, out_specs=P(None, row, col), check_vma=False
    )
```
